128 devices in a mesh: ctx: 32 (over z, x_lo, y), tp: 4 (over x_hi, core).
Axes of the slice: x: 4 (x_hi: 2, x_lo: 2; x = x_hi * 2 + x_lo), y: 4, z: 4, core: 2. Of those that a mesh axis runs over, the one named last changes fastest.
Arguments:
- queries: bfloat16 [24576, 2048], P('ctx', 'tp'), may hold values from -6 to 6
- keys: bfloat16 [24576, 2048], P('ctx', 'tp'), may hold values from -6 to 6
- values: bfloat16 [24576, 2048], P('ctx', 'tp'), may hold values from -6 to 6
- out_grad: bfloat16 [24576, 2048], P('ctx', 'tp'), may hold values from -6 to 6
- key_blocks: int32 [96, 16], replicated, may hold values from -1 to 95, as said below
- target_counts: int32 [96], replicated, may hold values from 0 to 128, as said below
Outputs:
- query_grad: bfloat16 [24576, 2048], P('ctx', 'tp')
- key_grad: bfloat16 [24576, 2048], P('ctx', 'tp')
- value_grad: bfloat16 [24576, 2048], P('ctx', 'tp')
The draws below stay inside these ranges and needn't reach their ends.
Inputs may be any that keep to these rules, and one draw needn't show every extreme that they name: `key_blocks`: entry 0 of row b is b itself; the other entries are distinct blocks k with b - 24 <= k < b, or -1 for an empty slot; a row has empty slots only where fewer than 15 such blocks exist. The last target_counts[b] events of block b are targets: no other event reads them as keys.
All inputs are finite; a program needn't handle non-finite values.
Results may differ from the reference program's by a relative error of at most 0.005.
Values may be sent and summed in bfloat16 or wider, within the bound.
No kernel may reach another device: no remote copies, remote signals or barrier semaphores. Data moves between devices by JAX's collectives and lax.ppermute only.
A program may use at most 64 MiB of HBM per device.

```python
import math
import jax
import jax.numpy as jnp
from jax import lax

HEADS = 16
HEAD = 128
BLK = 256
KPB = 16
BPD = 3
SPAN_TILE_COUNT = 96
TOKENS = 24576
REACH = 8


def draw_key_blocks(key, part):
    key = jax.random.fold_in(key, 11)
    hot_draw, stochastic_ranking_numbers = jax.random.split(key)
    holder_processors = jnp.arange(SPAN_TILE_COUNT, dtype=jnp.int32) // BPD
    frequent_marker_list = jax.random.randint(hot_draw, (SPAN_TILE_COUNT // BPD,), 0, 4) == 0
    frequent_extra_weight = jnp.where(frequent_marker_list[holder_processors], 4096, 0).astype(jnp.int32)
    initial_ranking_number = jax.random.randint(stochastic_ranking_numbers, (SPAN_TILE_COUNT, SPAN_TILE_COUNT), 0, 1024) + frequent_extra_weight[None, :]
    row_index = jnp.arange(SPAN_TILE_COUNT, dtype=jnp.int32)[:, None]
    col_index = jnp.arange(SPAN_TILE_COUNT, dtype=jnp.int32)[None, :]
    eligible_marker = (col_index < row_index) & (col_index >= row_index - REACH * BPD)
    scores = jnp.where(eligible_marker, initial_ranking_number * SPAN_TILE_COUNT + col_index, -1 - col_index)
    top_scores, top_ids = lax.top_k(scores, KPB - 1)
    chosen = jnp.where(top_scores >= 0, top_ids, -1).astype(jnp.int32)
    own_ids = jnp.arange(SPAN_TILE_COUNT, dtype=jnp.int32)[:, None]
    return jnp.concatenate([own_ids, chosen], axis=1).astype(jnp.int32)


def draw_target_counts(key, part):
    key = jax.random.fold_in(key, 7)
    count_draw, place_draw = jax.random.split(key)
    counts = jax.random.randint(count_draw, (SPAN_TILE_COUNT,), 0, BLK // 2 + 1)
    places = jax.random.permutation(place_draw, SPAN_TILE_COUNT)
    counts = counts.at[places[0]].set(BLK // 2)
    counts = counts.at[places[1]].set(0)
    return counts.astype(jnp.int32)


def block_levels(stream_key, shape, cuts, least, top_value):
    gain = 1.0
    for position, parts in cuts:
        steps = jax.random.uniform(jax.random.fold_in(jax.random.fold_in(stream_key, 6), position), (parts,), jnp.float32, least / len(cuts), top_value / len(cuts))
        gain = gain * jnp.repeat(jnp.exp(steps), shape[position] // parts).reshape((-1,) + (1,) * (len(shape) - 1 - position))
    return gain


def gaussian(rng, shape, deviation, most, cuts=(), kind=jnp.bfloat16):
    level = block_levels(rng, shape, cuts, -0.22, 0.18) if cuts else 1.0
    values = jax.random.normal(rng, shape, jnp.float32) * deviation * level
    return jnp.minimum(jnp.maximum(values, -most), most).astype(kind)


def setup_inputs(seed: int = 0) -> dict:
    key_list = jax.random.split(jax.random.key(seed), 7)
    return {
        "queries": gaussian(key_list[0], (TOKENS, HEADS * HEAD), 1.0, 6.0, ((0, 32), (1, 4))),
        "keys": gaussian(key_list[1], (TOKENS, HEADS * HEAD), 1.0, 6.0, ((0, 32), (1, 4))),
        "values": gaussian(key_list[2], (TOKENS, HEADS * HEAD), 1.0, 6.0, ((0, 32), (1, 4))),
        "out_grad": gaussian(key_list[3], (TOKENS, HEADS * HEAD), 1.0, 6.0, ((0, 32), (1, 4))),
        "key_blocks": draw_key_blocks(jax.random.fold_in(key_list[6], 71), 0),
        "target_counts": draw_target_counts(jax.random.fold_in(key_list[6], 71), 0),
    }


def block_mask(query_id, key_id, target_counts):
    row_index = jnp.arange(BLK, dtype=jnp.int32)[:, None]
    col_index = jnp.arange(BLK, dtype=jnp.int32)[None, :]
    own_targets = target_counts[query_id]
    key_targets = target_counts[key_id]
    diagonal = (col_index <= row_index) & ((col_index < BLK - own_targets) | (col_index == row_index))
    earlier = jnp.broadcast_to(col_index < BLK - key_targets, diagonal.shape)
    return jnp.where(query_id == key_id, diagonal, earlier).astype(jnp.float32)

def tile_grads(query_tile, grad_tile, key_tile, value_tile, allowed):
    head_factor = 1.0 / math.sqrt(HEAD)
    norm_scale = 1.0 / math.sqrt(KPB * BLK)
    query_wide = query_tile.astype(jnp.float32)
    grad_wide = grad_tile.astype(jnp.float32)
    key_wide = key_tile.astype(jnp.float32)
    value_wide = value_tile.astype(jnp.float32)
    scores = jnp.einsum('ihd,jhd->hij', query_wide, key_wide) * head_factor
    sigmoid_part = jax.nn.sigmoid(scores)
    gated = allowed[None] * norm_scale
    weights = (scores * sigmoid_part * gated).astype(jnp.bfloat16)
    weight_grad = jnp.einsum('ihd,jhd->hij', grad_wide, value_wide)
    score_grad = (weight_grad * gated * sigmoid_part * (1.0 + scores * (1.0 - sigmoid_part))).astype(jnp.bfloat16)
    score_wide = score_grad.astype(jnp.float32)
    query_part = jnp.einsum('hij,jhd->ihd', score_wide, key_wide) * head_factor
    key_part = jnp.einsum('hij,ihd->jhd', score_wide, query_wide) * head_factor
    payload_portion = jnp.einsum('hij,ihd->jhd', weights.astype(jnp.float32), grad_wide)
    return (query_part, key_part, payload_portion)

def reference(queries, keys, values, out_grad, key_blocks, target_counts):
    block_shape = (SPAN_TILE_COUNT, BLK, HEADS, HEAD)
    query_blocks = queries.reshape(block_shape)
    key_tiles = keys.reshape(block_shape)
    value_tiles = values.reshape(block_shape)
    grad_blocks = out_grad.reshape(block_shape)

    def per_query(state, block_id):
        key_acc, value_acc = state
        query_acc = jnp.zeros((BLK, HEADS, HEAD), jnp.float32)
        for slot in range(KPB):
            listed_id = key_blocks[block_id, slot]
            slot_valid = (listed_id >= 0).astype(jnp.float32)
            safe_id = jnp.maximum(listed_id, 0).astype(jnp.int32)
            allowed = block_mask(block_id, safe_id, target_counts) * slot_valid
            query_part, key_part, payload_portion = tile_grads(query_blocks[block_id], grad_blocks[block_id], key_tiles[safe_id], value_tiles[safe_id], allowed)
            query_acc = query_acc + query_part
            key_acc = key_acc.at[safe_id].add(key_part)
            value_acc = value_acc.at[safe_id].add(payload_portion)
        return ((key_acc, value_acc), query_acc)
    empty = jnp.zeros(block_shape, jnp.float32)
    (key_acc, value_acc), query_acc = lax.scan(per_query, (empty, empty), jnp.arange(SPAN_TILE_COUNT, dtype=jnp.int32))
    flat = (TOKENS, HEADS * HEAD)
    return (query_acc.reshape(flat).astype(jnp.bfloat16), key_acc.reshape(flat).astype(jnp.bfloat16), value_acc.reshape(flat).astype(jnp.bfloat16))
```

```python
import functools
import math

import jax
import jax.numpy as jnp
from jax import lax
from jax.experimental import pallas as pl
from jax.experimental.pallas import tpu as pltpu
from jax.sharding import PartitionSpec as P

F32, BF = jnp.float32, jnp.bfloat16
HEAD, BLK, KPB = 128, 256, 16
PLANE, HALF = 24, 12
AXES = ("ctx", "tp")
U_SCALE = 0.5 / math.sqrt(HEAD)
V_SCALE = 1.0 / math.sqrt(KPB * BLK)
QK_SCALE = 0.5 * V_SCALE / math.sqrt(HEAD)
GROUP = 6
CLASSES = (160, 192, 224, 256)
ENTRIES = 360
DUMMY_Q, DUMMY_K = 24, 36
VMEM = pl.BlockSpec(memory_space=pltpu.VMEM)
SMEM = pl.BlockSpec(memory_space=pltpu.SMEM)
ANY = pl.BlockSpec(memory_space=pl.ANY)


def place(z, x, y, hi, core):
    return (z * 8 + x * 4 + y % 4) * 4 + hi * 2 + core


DEVICES = [
    (z, x, y, hi, core)
    for z in range(4)
    for x in range(2)
    for y in range(4)
    for hi in range(2)
    for core in range(2)
]


def to_heads(d):
    return [(place(z, x, y, hi, c), place(z, c, y + d, hi, x)) for z, x, y, hi, c in DEVICES]


def from_heads(d):
    return [(j, i) for i, j in to_heads(d)]


OTHER_CORE = [(place(z, x, y, hi, c), place(z, x, y, hi, 1 - c)) for z, x, y, hi, c in DEVICES]
ALONG_Z = [
    (place(z, x, y, hi, c), place(z + 2 * c - 1, x, y, hi, c))
    for z, x, y, hi, c in DEVICES
    if 0 <= z + 2 * c - 1 < 4
]
BACK_Z = [(j, i) for i, j in ALONG_Z]


def nt(a, b):
    return lax.dot_general(a, b, (((1,), (1,)), ((), ())), preferred_element_type=F32)


def nn(a, b):
    return lax.dot_general(a, b, (((1,), (0,)), ((), ())), preferred_element_type=F32)


def tn(a, b):
    return lax.dot_general(a, b, (((0,), (0,)), ((), ())), preferred_element_type=F32)


def split_kernel(at, q, g, k, v, *outs):
    y, x = at[0], at[1]
    for d in range(4):
        lanes = pl.ds(pl.multiple_of(lax.rem(y + d, 4) * HEAD, HEAD), HEAD)

        def put(target, pair, lanes=lanes):
            for n, src in enumerate(pair):
                target[n] = src[:, lanes]

        for first, pair in ((0, (q, g)), (1, (k, v))):

            @pl.when(x == first)
            def _(d=d, pair=pair):
                put(outs[d], pair)

            @pl.when(x != first)
            def _(d=d, pair=pair):
                put(outs[4 + d], pair)


def pair_grads(scores, weight_grad, allowed):
    u = scores * U_SCALE
    t = jnp.tanh(u)
    p = jnp.where(allowed, 1.0 + t, 0.0)
    w = u * p
    slope = p + w * (1.0 - t)
    return w.astype(BF), (weight_grad * slope).astype(BF)


def main_kernel(at, tab, cls, nvd, *refs):
    r1, r2 = refs[0:4], refs[4:8]
    beside, across = refs[8:10]
    dq_own, dk_own, dv_own, beside_out, across_out = refs[10:15]
    qs, gs, ks, vs, dqa, dka, dva, sems = refs[15:]
    core, groups = at[2], at[3]

    def copies(own):
        qg, kv = ((r1, r2), (r2, r1))[own]
        out = []
        for d in range(4):
            rows = pl.ds(3 * d, 3)
            out += [
                (qg[d].at[0], qs.at[rows]),
                (qg[d].at[1], gs.at[rows]),
                (kv[d].at[0], ks.at[rows]),
                (kv[d].at[1], vs.at[rows]),
            ]
        out += [(beside.at[0], ks.at[pl.ds(12, 12)]), (beside.at[1], vs.at[pl.ds(12, 12)])]
        if own == 0:
            out += [(across.at[0], qs.at[pl.ds(12, 12)]), (across.at[1], gs.at[pl.ds(12, 12)])]
        else:
            out += [(across.at[0], ks.at[pl.ds(24, 12)]), (across.at[1], vs.at[pl.ds(24, 12)])]
        return [pltpu.make_async_copy(a, b, sems.at[i]) for i, (a, b) in enumerate(out)]

    for own in range(2):

        @pl.when(core == own)
        def _(own=own):
            for copy in copies(own):
                copy.start()

    dqa[...] = jnp.zeros_like(dqa)
    dka[...] = jnp.zeros_like(dka)
    dva[...] = jnp.zeros_like(dva)
    zero = jnp.zeros((BLK, HEAD), BF)
    qs[DUMMY_Q], gs[DUMMY_Q], ks[DUMMY_K], vs[DUMMY_K] = zero, zero, zero, zero

    for own in range(2):

        @pl.when(core == own)
        def _(own=own):
            for copy in copies(own):
                copy.wait()

    def work(items, rows):
        made = []
        for q, k, mask in items:
            key, value, query, grad = ks[k, :rows], vs[k, :rows], qs[q], gs[q]
            made.append((q, k, mask, key, query, grad, nt(key, query), nt(value, grad)))
        for q, k, mask, key, query, grad, scores, weight_grad in made:
            w, sg = pair_grads(scores, weight_grad, mask)
            dva[k, :rows] += nn(w, grad)
            dka[k, :rows] += nn(sg, query)
            dqa[q] += tn(key, sg)

    def own_group(g, _):
        items = []
        row = lax.broadcasted_iota(jnp.int32, (BLK, BLK), 0)
        col = lax.broadcasted_iota(jnp.int32, (BLK, BLK), 1)
        for i in range(4):
            slot = g * 4 + i
            items.append((slot, slot, (row == col) | ((row < col) & (row < nvd[slot]))))
        work(items, BLK)
        return 0

    lax.fori_loop(0, 3, own_group, 0)

    def group(g, _):
        for c, rows in enumerate(CLASSES):

            @pl.when(cls[g] == c)
            def _(rows=rows):
                row = lax.broadcasted_iota(jnp.int32, (rows, BLK), 0)
                items = []
                for i in range(GROUP):
                    e = tab[g * GROUP + i]
                    items.append((e & 31, (e >> 5) & 63, row < ((e >> 11) & 511)))
                work(items, rows)

        return 0

    lax.fori_loop(0, groups, group, 0)

    def finish(s, _):
        dq_own[s] = dqa[s].T * QK_SCALE
        dk_own[s] = dka[s] * QK_SCALE
        dv_own[s] = dva[s] * V_SCALE
        beside_out[0, s] = (dka[12 + s] * QK_SCALE).astype(BF)
        beside_out[1, s] = (dva[12 + s] * V_SCALE).astype(BF)

        @pl.when(core == 0)
        def _():
            across_out[0, s] = (dqa[12 + s].T * QK_SCALE).astype(BF)
            across_out[1, s] = jnp.zeros((BLK, HEAD), BF)

        @pl.when(core == 1)
        def _():
            across_out[0, s] = (dka[24 + s] * QK_SCALE).astype(BF)
            across_out[1, s] = (dva[24 + s] * V_SCALE).astype(BF)

        return 0

    lax.fori_loop(0, 12, finish, 0)


def sum_kernel(at, dq, dk, dv, beside, across, *outs):
    core = at[2]
    for d in range(4):
        for m in range(3):
            s = 3 * d + m
            near = (beside[0, s].astype(F32), beside[1, s].astype(F32))
            far = (across[0, s].astype(F32), across[1, s].astype(F32))
            first = core == 0
            outs[d][0, m] = (dq[s] + jnp.where(first, far[0], 0.0)).astype(BF)
            outs[d][1, m] = (dk[s] + near[0] + jnp.where(first, 0.0, far[0])).astype(BF)
            outs[d][2, m] = (dv[s] + near[1] + jnp.where(first, 0.0, far[1])).astype(BF)


def join_kernel(at, *refs):
    y = at[0]
    for d in range(4):
        lanes = pl.ds(pl.multiple_of(lax.rem(y + d, 4) * HEAD, HEAD), HEAD)
        for n in range(3):
            refs[4 + n][:, lanes] = refs[d][n]


def call(kernel, outs, ins, scratch=(), limit=48, **kw):
    return pl.pallas_call(
        kernel,
        out_shape=outs,
        in_specs=ins,
        out_specs=[VMEM] * len(outs),
        scratch_shapes=scratch,
        compiler_params=pltpu.CompilerParams(vmem_limit_bytes=limit * 2**20),
        **kw,
    )


def tables(key_blocks, target_counts, z, y, core):
    def slot(t):
        return lax.rem(y + 4 - (t % HALF) // 3, 4) * 3 + t % 3

    own = lax.dynamic_slice(key_blocks, (PLANE * z + HALF * core, 0), (HALF, KPB))
    after = lax.dynamic_slice(key_blocks, (jnp.minimum(PLANE * (z + 1), 84), 0), (HALF, KPB))
    kid = jnp.concatenate([own, after])[:, 1:]
    index = jnp.arange(2 * HALF, dtype=jnp.int32)[:, None]
    q_valid = (index < HALF) | ((core == 0) & (z < 3))
    plane = jnp.maximum(kid, 0) // PLANE
    valid = q_valid & (kid >= 0) & ((core == 1) | (plane == z))
    t = jnp.maximum(kid, 0) - PLANE * plane
    ks = slot(t) + jnp.where(plane == z, jnp.where(t // HALF == core, 0, 12), 24)
    qs = jnp.broadcast_to(slot(index % HALF) + jnp.where(index < HALF, 0, 12), kid.shape)
    ids = jnp.arange(96, dtype=jnp.int32)
    counts = jnp.sum(jnp.where(kid[..., None] == ids, target_counts, 0), -1)
    rows = BLK - counts
    cls = jnp.clip((rows + 31) // 32 - 5, 0, 3)
    value = (qs | (ks << 5) | (rows << 11) | (cls << 20)).reshape(-1)
    order = jnp.where(valid, cls, 4).reshape(-1)
    n = jnp.arange(ENTRIES, dtype=jnp.int32)
    before = (order[None, :] < order[:, None]) | (
        (order[None, :] == order[:, None]) & (n[None, :] < n[:, None])
    )
    rank = jnp.sum(before.astype(jnp.int32), 1)
    total = jnp.sum(valid.astype(jnp.int32))
    tab = jnp.sum(jnp.where(rank[None, :] == n[:, None], value[None, :], 0), 1)
    tab = jnp.where(n < total, tab, DUMMY_Q | (DUMMY_K << 5))
    cls_of = jnp.max((tab >> 20).reshape(-1, GROUP), 1)
    s = jnp.arange(HALF, dtype=jnp.int32)
    block = PLANE * z + HALF * core + lax.rem(y + 4 - s // 3, 4) * 3 + s % 3
    nvd = BLK - jnp.sum(jnp.where(block[:, None] == ids, target_counts, 0), -1)
    return tab, cls_of, nvd, (total + GROUP - 1) // GROUP


def body(queries, keys, values, out_grad, key_blocks, target_counts):
    ctx, tp = lax.axis_index("ctx"), lax.axis_index("tp")
    z, x, y, core = ctx // 8, (ctx // 4) % 2, ctx % 4, tp % 2
    tab, cls, nvd, groups = tables(key_blocks, target_counts, z, y, core)
    at = jnp.stack([y, x, core, groups]).astype(jnp.int32)
    rows = queries.shape[0]
    piece = jax.ShapeDtypeStruct((2, rows, HEAD), BF)
    here = jnp.stack([y, x]).astype(jnp.int32)
    sent = call(split_kernel, [piece] * 8, [SMEM] + [VMEM] * 4, name="split")(
        here, queries, out_grad, keys, values
    )
    got = [lax.ppermute(sent[n], AXES, to_heads(n % 4)) for n in range(8)]
    got = [g.reshape(2, 3, BLK, HEAD) for g in got]
    r1, r2 = jnp.concatenate(got[:4], 1), jnp.concatenate(got[4:], 1)
    across = lax.ppermute(r1, AXES, ALONG_Z)
    beside = lax.ppermute(jnp.where(core == 0, r2, r1), AXES, OTHER_CORE)
    half = jax.ShapeDtypeStruct((HALF, BLK, HEAD), F32)
    two = jax.ShapeDtypeStruct((2, HALF, BLK, HEAD), BF)
    dq, dk, dv, beside_out, across_out = call(
        main_kernel,
        [half, half, half, two, two],
        [SMEM] * 4 + [ANY] * 10,
        [
            pltpu.VMEM((25, BLK, HEAD), BF),
            pltpu.VMEM((25, BLK, HEAD), BF),
            pltpu.VMEM((37, BLK, HEAD), BF),
            pltpu.VMEM((37, BLK, HEAD), BF),
            pltpu.VMEM((25, HEAD, BLK), F32),
            pltpu.VMEM((37, BLK, HEAD), F32),
            pltpu.VMEM((37, BLK, HEAD), F32),
            pltpu.SemaphoreType.DMA((20,)),
        ],
        name="grads",
    )(at, tab, cls, nvd, *got, beside, across)
    beside = lax.ppermute(beside_out, AXES, OTHER_CORE)
    across = lax.ppermute(across_out, AXES, BACK_Z)
    three = jax.ShapeDtypeStruct((3, 3, BLK, HEAD), BF)
    sums = call(sum_kernel, [three] * 4, [SMEM] + [VMEM] * 5, name="sums")(
        at, dq, dk, dv, beside, across
    )
    back = [lax.ppermute(s.reshape(3, rows, HEAD), AXES, from_heads(d)) for d, s in enumerate(sums)]
    out = jax.ShapeDtypeStruct(queries.shape, BF)
    return tuple(call(join_kernel, [out] * 3, [SMEM] + [VMEM] * 4, name="join")(here, *back))


def solution(mesh):
    in_specs = (P("ctx", "tp"),) * 4 + (P(), P())
    return jax.shard_map(
        body, mesh=mesh, in_specs=in_specs, out_specs=(P("ctx", "tp"),) * 3, check_vma=False
    )
```

```python
import functools
import math

import jax
import jax.numpy as jnp
from jax import lax
from jax.experimental import pallas as pl
from jax.experimental.pallas import tpu as pltpu
from jax.sharding import PartitionSpec as P

F32, BF = jnp.float32, jnp.bfloat16
HEAD, BLK, KPB = 128, 256, 16
PLANE, HALF = 24, 12
AXES = ("ctx", "tp")
U_SCALE = 0.5 / math.sqrt(HEAD)
V_SCALE = 1.0 / math.sqrt(KPB * BLK)
QK_SCALE = 0.5 * V_SCALE / math.sqrt(HEAD)
GROUP = 6
CLASSES = (160, 192, 224, 256)
ENTRIES = 180
LISTED = ENTRIES // GROUP
DUMMY = (24, 12)
VMEM = pl.BlockSpec(memory_space=pltpu.VMEM)
SMEM = pl.BlockSpec(memory_space=pltpu.SMEM)
ANY = pl.BlockSpec(memory_space=pl.ANY)


def place(z, x, y, hi, core):
    return (z * 8 + x * 4 + y % 4) * 4 + hi * 2 + core


DEVICES = [
    (z, x, y, hi, core)
    for z in range(4)
    for x in range(2)
    for y in range(4)
    for hi in range(2)
    for core in range(2)
]


def to_heads(d):
    return [(place(z, x, y, hi, c), place(z, c, y + d, hi, x)) for z, x, y, hi, c in DEVICES]


def from_heads(d):
    return [(j, i) for i, j in to_heads(d)]


OTHER_CORE = [(place(z, x, y, hi, c), place(z, x, y, hi, 1 - c)) for z, x, y, hi, c in DEVICES]
TO_FIRST = [(place(z, x, y, hi, 1), place(z, x, y, hi, 0)) for z, x, y, hi, c in DEVICES if c]
TO_SECOND = [(j, i) for i, j in TO_FIRST]
ALONG_Z = [
    (place(z, x, y, hi, c), place(z + 2 * c - 1, x, y, hi, c))
    for z, x, y, hi, c in DEVICES
    if 0 <= z + 2 * c - 1 < 4
]
BACK_Z = [(j, i) for i, j in ALONG_Z]
BACK_Z_SECOND = [(j, i) for j, i in BACK_Z if i % 2]


def nt(a, b):
    return lax.dot_general(a, b, (((1,), (1,)), ((), ())), preferred_element_type=F32)


def nn(a, b):
    return lax.dot_general(a, b, (((1,), (0,)), ((), ())), preferred_element_type=F32)


def tn(a, b):
    return lax.dot_general(a, b, (((0,), (0,)), ((), ())), preferred_element_type=F32)


def split_kernel(first_round, at, q, g, k, v, *refs):
    outs, sems = refs[:4], refs[4]
    y, x = at[0], at[1]

    def copies(pair):
        made = []
        for d in range(4):
            lanes = pl.ds(pl.multiple_of(lax.rem(y + d, 4) * HEAD, HEAD), HEAD)
            for n in range(2):
                made.append(
                    pltpu.make_async_copy(
                        pair[n].at[:, lanes], outs[d].at[n], sems.at[2 * d + n]
                    )
                )
        return made

    for side, pair in ((0, (q, g)), (1, (k, v))):

        @pl.when(x == (side if first_round else 1 - side))
        def _(pair=pair):
            made = copies(pair)
            for copy in made:
                copy.start()
            for copy in made:
                copy.wait()


def gather_kernel(*refs):
    ins, out, sems = refs[:4], refs[4], refs[5]
    made = [
        pltpu.make_async_copy(ins[d], out.at[:, pl.ds(3 * d, 3)], sems.at[d]) for d in range(4)
    ]
    for copy in made:
        copy.start()
    for copy in made:
        copy.wait()


def pair_grads(scores, weight_grad, allowed):
    u = scores * U_SCALE
    t = jnp.tanh(u)
    p = jnp.where(allowed, 1.0 + t, 0.0)
    w = u * p
    slope = p + w * (1.0 - t)
    return w.astype(BF), (weight_grad * slope).astype(BF)


def pairs_kernel(phase, at, tab, cls, nvd, *refs):
    r1, r2 = refs[0:4], refs[4:8]
    extra = refs[8:10] if phase else refs[8:11]
    refs = refs[10:] if phase else refs[11:]
    if phase:
        dq_out, dk_out, dv_out = refs[:3]
        refs = refs[3:]
        qs, gs, ks, vs, dqa, dka, dva, s1, s2, sems = refs
    else:
        p1_out, p2_out, s1_out, s2_out, beside_out = refs[:5]
        qs, gs, ks, vs, dqa, dka, dva, sems = refs[5:]
    core, groups = at[2], at[3 + phase]
    low, high = pl.ds(0, HALF), pl.ds(HALF, HALF)

    def copies(own):
        qg, kv = ((r1, r2), (r2, r1))[own]
        out = []
        for d in range(4):
            rows = pl.ds(3 * d, 3)
            if phase == 1 or own == 1:
                out += [(qg[d].at[0], qs.at[rows]), (qg[d].at[1], gs.at[rows])]
            if phase == 1 or own == 0:
                out += [(kv[d].at[0], ks.at[rows]), (kv[d].at[1], vs.at[rows])]
        if phase == 0:
            across, beside = extra[0], extra[1 + own]
            out += [(beside.at[0], ks.at[high]), (beside.at[1], vs.at[high])]
            if own == 0:
                out += [(across.at[0], qs.at[low]), (across.at[1], gs.at[low])]
            else:
                out += [(across.at[0], ks.at[low]), (across.at[1], vs.at[low])]
        return [pltpu.make_async_copy(a, b, sems.at[i]) for i, (a, b) in enumerate(out)]

    def late():
        return [
            pltpu.make_async_copy(extra[0], s1, sems.at[20]),
            pltpu.make_async_copy(extra[1], s2, sems.at[21]),
        ]

    for own in range(2):

        @pl.when(core == own)
        def _(own=own):
            for copy in copies(own):
                copy.start()

    if phase:
        for copy in late():
            copy.start()
    dqa[...] = jnp.zeros_like(dqa)
    dka[...] = jnp.zeros_like(dka)
    dva[...] = jnp.zeros_like(dva)
    zero = jnp.zeros((BLK, HEAD), BF)
    dummy = DUMMY[phase]
    qs[HALF], gs[HALF], ks[dummy], vs[dummy] = zero, zero, zero, zero

    for own in range(2):

        @pl.when(core == own)
        def _(own=own):
            for copy in copies(own):
                copy.wait()

    def work(items, rows):
        made = []
        for q, k, mask in items:
            key, value, query, grad = ks[k, :rows], vs[k, :rows], qs[q], gs[q]
            made.append((q, k, mask, key, query, grad, nt(key, query), nt(value, grad)))
        for q, k, mask, key, query, grad, scores, weight_grad in made:
            w, sg = pair_grads(scores, weight_grad, mask)
            dva[k, :rows] += nn(w, grad)
            dka[k, :rows] += nn(sg, query)
            dqa[q] += tn(key, sg)

    def own_group(g, _):
        items = []
        row = lax.broadcasted_iota(jnp.int32, (BLK, BLK), 0)
        col = lax.broadcasted_iota(jnp.int32, (BLK, BLK), 1)
        for i in range(4):
            slot = g * 4 + i
            items.append((slot, slot, (row == col) | ((row < col) & (row < nvd[slot]))))
        work(items, BLK)
        return 0

    if phase:
        lax.fori_loop(0, 3, own_group, 0)

    def group(g, _):
        for c, rows in enumerate(CLASSES):

            @pl.when(cls[phase * LISTED + g] == c)
            def _(rows=rows):
                row = lax.broadcasted_iota(jnp.int32, (rows, BLK), 0)
                items = []
                for i in range(GROUP):
                    e = tab[phase * ENTRIES + g * GROUP + i]
                    items.append((e & 15, (e >> 4) & 31, row < ((e >> 9) & 511)))
                work(items, rows)

        return 0

    lax.fori_loop(0, groups, group, 0)

    if phase:
        for copy in late():
            copy.wait()

    def finish(s, _):
        dq, dk, dv = dqa[s].T * QK_SCALE, dka[s] * QK_SCALE, dva[s] * V_SCALE
        if phase:
            dq_out[s] = dq + jnp.where(core == 1, s1[s], 0.0)
            dk_out[s] = dk + jnp.where(core == 0, s1[s], 0.0)
            dv_out[s] = dv + jnp.where(core == 0, s2[s], 0.0)
        else:
            p1_out[s] = jnp.where(core == 0, dq, dk).astype(BF)
            p2_out[s] = dv.astype(BF)
            s1_out[s] = jnp.where(core == 0, dk, dq)
            s2_out[s] = dv
            beside_out[0, s] = (dka[HALF + s] * QK_SCALE).astype(BF)
            beside_out[1, s] = (dva[HALF + s] * V_SCALE).astype(BF)
        return 0

    lax.fori_loop(0, HALF, finish, 0)


def piped(ins, shapes, in_sems, outs, staged, out_sems, compute):
    def coming(d):
        rows = pl.ds(3 * d, 3)
        return [
            pltpu.make_async_copy(
                src.at[:, rows] if four else src.at[rows],
                dst.at[:, rows] if four else dst.at[rows],
                in_sems.at[d, n],
            )
            for n, (src, dst, four) in enumerate(zip(ins, shapes[0], shapes[1]))
        ]

    def going(d):
        return pltpu.make_async_copy(staged.at[d], outs[d], out_sems.at[d])

    for d in range(4):
        for copy in coming(d):
            copy.start()
    for d in range(4):
        for copy in coming(d):
            copy.wait()
        compute(d)
        going(d).start()
    for d in range(4):
        going(d).wait()


def dq_kernel(at, dq, across, o0, o1, o2, o3, dq_v, across_v, staged, in_sems, out_sems):
    first = at[2] == 0

    def compute(d):
        for m in range(3):
            s = 3 * d + m
            far = across_v[s].astype(F32)
            staged[d, m] = (dq_v[s] + jnp.where(first, far, 0.0)).astype(BF)

    piped(
        (dq, across), ((dq_v, across_v), (0, 0)), in_sems, (o0, o1, o2, o3), staged, out_sems, compute
    )


def dkv_kernel(at, *refs):
    ins, outs = refs[:5], refs[5:9]
    bufs, (staged, in_sems, out_sems) = refs[9:14], refs[14:]
    dk, dv, beside, a1, a2 = bufs
    first = at[2] == 0

    def compute(d):
        for m in range(3):
            s = 3 * d + m
            for n, (own, far) in enumerate(((dk, a1), (dv, a2))):
                near = beside[n, s].astype(F32)
                far = jnp.where(first, 0.0, far[s].astype(F32))
                staged[d, n, m] = (own[s] + near + far).astype(BF)

    piped(ins, (bufs, (0, 0, 1, 0, 0)), in_sems, outs, staged, out_sems, compute)


def join_kernel(arrays, at, *refs):
    outs, sems = refs[4 : 4 + arrays], refs[-1]
    made = []
    for d in range(4):
        lanes = pl.ds(pl.multiple_of(lax.rem(at[0] + d, 4) * HEAD, HEAD), HEAD)
        for n in range(arrays):
            made.append(
                pltpu.make_async_copy(
                    refs[d].at[n], outs[n].at[:, lanes], sems.at[d * arrays + n]
                )
            )
    for copy in made:
        copy.start()
    for copy in made:
        copy.wait()


def call(kernel, outs, ins, scratch=(), limit=56, where=ANY, cost=None, **kw):
    return pl.pallas_call(
        kernel,
        out_shape=outs,
        in_specs=ins,
        out_specs=[where] * len(outs),
        scratch_shapes=scratch,
        compiler_params=pltpu.CompilerParams(vmem_limit_bytes=limit * 2**20),
        cost_estimate=cost,
        **kw,
    )


def table(qs, ks, valid, counts, dummy):
    rows = BLK - counts
    cls = jnp.clip((rows + 31) // 32 - 5, 0, 3)
    value = (qs | (ks << 4) | (rows << 9) | (cls << 18)).reshape(-1)
    order = jnp.where(valid, cls, 4).reshape(-1)
    n = jnp.arange(ENTRIES, dtype=jnp.int32)
    before = (order[None, :] < order[:, None]) | (
        (order[None, :] == order[:, None]) & (n[None, :] < n[:, None])
    )
    rank = jnp.sum(before.astype(jnp.int32), 1)
    total = jnp.sum(valid.astype(jnp.int32))
    tab = jnp.sum(jnp.where(rank[None, :] == n[:, None], value[None, :], 0), 1)
    tab = jnp.where(n < total, tab, HALF | (dummy << 4))
    return tab, jnp.max((tab >> 18).reshape(-1, GROUP), 1), (total + GROUP - 1) // GROUP


def tables(key_blocks, target_counts, z, y, core):
    def slot(t):
        return lax.rem(y + 4 - (t % HALF) // 3, 4) * 3 + t % 3

    ids = jnp.arange(96, dtype=jnp.int32)
    own = lax.dynamic_slice(key_blocks, (PLANE * z + HALF * core, 0), (HALF, KPB))[:, 1:]
    after = lax.dynamic_slice(key_blocks, (jnp.minimum(PLANE * (z + 1), 84), 0), (HALF, KPB))[:, 1:]
    qs = jnp.broadcast_to(slot(jnp.arange(HALF, dtype=jnp.int32))[:, None], own.shape)
    made = []
    for phase in range(2):
        kid = own if phase else jnp.where(core == 0, after, own)
        plane = jnp.maximum(kid, 0) // PLANE
        t = jnp.maximum(kid, 0) - PLANE * plane
        same = (plane == z) & (t // HALF == core)
        if phase:
            valid, ks = (kid >= 0) & same, slot(t)
        else:
            valid = (kid >= 0) & jnp.where(core == 0, (z < 3) & (plane == z), ~same)
            other = (plane == z) & (t // HALF != core)
            ks = slot(t) + jnp.where(other, HALF, 0)
        counts = jnp.sum(jnp.where(kid[..., None] == ids, target_counts, 0), -1)
        made.append(table(qs, ks, valid, counts, DUMMY[phase]))
    s = jnp.arange(HALF, dtype=jnp.int32)
    block = PLANE * z + HALF * core + lax.rem(y + 4 - s // 3, 4) * 3 + s % 3
    nvd = BLK - jnp.sum(jnp.where(block[:, None] == ids, target_counts, 0), -1)
    return made, nvd


def pairs_cost(pairs):
    return pl.CostEstimate(
        flops=pairs * 10 * BLK * BLK * HEAD, bytes_accessed=12 * 2**20, transcendentals=pairs * BLK * BLK
    )


def body(queries, keys, values, out_grad, key_blocks, target_counts):
    ctx, tp = lax.axis_index("ctx"), lax.axis_index("tp")
    z, x, y, core = ctx // 8, (ctx // 4) % 2, ctx % 4, tp % 2
    here = jnp.stack([y, x]).astype(jnp.int32)
    rows = queries.shape[0]
    shape = jax.ShapeDtypeStruct
    dma = lambda *n: pltpu.SemaphoreType.DMA(n)

    def split(first_round):
        return call(
            functools.partial(split_kernel, first_round),
            [shape((2, rows, HEAD), BF)] * 4,
            [SMEM] + [ANY] * 4,
            [dma(8)],
            limit=56,
            name="split",
        )(here, queries, out_grad, keys, values)

    def send(pieces, pairs):
        return [lax.ppermute(p, AXES, pairs(d)) for d, p in enumerate(pieces)]

    two = shape((2, HALF, BLK, HEAD), BF)

    def gather(pieces):
        return call(gather_kernel, [two], [ANY] * 4, [dma(4)], limit=56, name="gather")(*pieces)[0]

    def blocks(pieces):
        return [p.reshape(2, 3, BLK, HEAD) for p in pieces]

    r1 = blocks(send(split(True), to_heads))
    r2 = blocks(send(split(False), to_heads))
    all1 = gather(r1)
    across = lax.ppermute(all1, AXES, ALONG_Z)
    to_first = lax.ppermute(all1, AXES, TO_FIRST)
    to_second = lax.ppermute(gather(r2), AXES, TO_SECOND)

    (far, own), nvd = tables(key_blocks, target_counts, z, y, core)
    at = jnp.stack([y, x, core, far[2], own[2]]).astype(jnp.int32)
    tab = jnp.concatenate([far[0], own[0]])
    cls = jnp.concatenate([far[1], own[1]])
    half, half16 = shape((HALF, BLK, HEAD), F32), shape((HALF, BLK, HEAD), BF)

    def scratch(k):
        return [
            pltpu.VMEM((HALF + 1, BLK, HEAD), BF),
            pltpu.VMEM((HALF + 1, BLK, HEAD), BF),
            pltpu.VMEM((k + 1, BLK, HEAD), BF),
            pltpu.VMEM((k + 1, BLK, HEAD), BF),
            pltpu.VMEM((HALF + 1, HEAD, BLK), F32),
            pltpu.VMEM((k + 1, BLK, HEAD), F32),
            pltpu.VMEM((k + 1, BLK, HEAD), F32),
        ]

    p1, p2, s1, s2, beside = call(
        functools.partial(pairs_kernel, 0),
        [half16, half16, half, half, two],
        [SMEM] * 4 + [ANY] * 11,
        scratch(PLANE) + [dma(22)],
        where=VMEM,
        cost=pairs_cost(139),
        name="far",
    )(at, tab, cls, nvd, *r1, *r2, across, to_first, to_second)
    p1 = lax.ppermute(p1, AXES, BACK_Z)
    p2 = lax.ppermute(p2, AXES, BACK_Z_SECOND)
    beside = lax.ppermute(beside, AXES, OTHER_CORE)
    dq, dk, dv = call(
        functools.partial(pairs_kernel, 1),
        [half, half, half],
        [SMEM] * 4 + [ANY] * 10,
        scratch(HALF) + [pltpu.VMEM((HALF, BLK, HEAD), F32)] * 2 + [dma(22)],
        where=VMEM,
        cost=pairs_cost(60),
        name="own",
    )(at, tab, cls, nvd, *r1, *r2, s1, s2)
    v3, v3h = pltpu.VMEM((HALF, BLK, HEAD), F32), pltpu.VMEM((HALF, BLK, HEAD), BF)
    v4 = pltpu.VMEM((2, HALF, BLK, HEAD), BF)
    dq_sent = call(
        dq_kernel,
        [shape((3, BLK, HEAD), BF)] * 4,
        [SMEM] + [ANY] * 2,
        [v3, v3h, pltpu.VMEM((4, 3, BLK, HEAD), BF), dma(4, 2), dma(4)],
        name="dq",
    )(at, dq, p1)
    dq_back = send([p.reshape(1, rows, HEAD) for p in dq_sent], from_heads)
    dkv_sent = call(
        dkv_kernel,
        [shape((2, 3, BLK, HEAD), BF)] * 4,
        [SMEM] + [ANY] * 5,
        [v3, v3, v4, v3h, v3h, pltpu.VMEM((4, 2, 3, BLK, HEAD), BF), dma(4, 5), dma(4)],
        name="dkv",
    )(at, dk, dv, beside, p1, p2)
    dkv_back = send([p.reshape(2, rows, HEAD) for p in dkv_sent], from_heads)
    out = shape(queries.shape, BF)

    def join(pieces, arrays):
        return call(
            functools.partial(join_kernel, arrays),
            [out] * arrays,
            [SMEM] + [ANY] * 4,
            [dma(4 * arrays)],
            limit=56,
            name="join",
        )(here, *pieces)

    return (*join(dq_back, 1), *join(dkv_back, 2))


def solution(mesh):
    in_specs = (P("ctx", "tp"),) * 4 + (P(), P())
    return jax.shard_map(
        body, mesh=mesh, in_specs=in_specs, out_specs=(P("ctx", "tp"),) * 3, check_vma=False
    )
```

```python
import functools
import math

import jax
import jax.numpy as jnp
from jax import lax
from jax.experimental import pallas as pl
from jax.experimental.pallas import tpu as pltpu
from jax.sharding import PartitionSpec as P

F32, BF = jnp.float32, jnp.bfloat16
HEAD, BLK, KPB = 128, 256, 16
PLANE, HALF = 24, 12
AXES = ("ctx", "tp")
U_SCALE = 0.5 / math.sqrt(HEAD)
V_SCALE = 1.0 / math.sqrt(KPB * BLK)
QK_SCALE = 0.5 * V_SCALE / math.sqrt(HEAD)
GROUP = 6
CLASSES = (160, 192, 224, 256)
ENTRIES = 180
LISTED = ENTRIES // GROUP
DUMMY = (24, 12)
VMEM = pl.BlockSpec(memory_space=pltpu.VMEM)
SMEM = pl.BlockSpec(memory_space=pltpu.SMEM)
ANY = pl.BlockSpec(memory_space=pl.ANY)


def place(z, x, y, hi, core):
    return (z * 8 + x * 4 + y % 4) * 4 + hi * 2 + core


DEVICES = [
    (z, x, y, hi, core)
    for z in range(4)
    for x in range(2)
    for y in range(4)
    for hi in range(2)
    for core in range(2)
]


def to_heads(d):
    return [(place(z, x, y, hi, c), place(z, c, y + d, hi, x)) for z, x, y, hi, c in DEVICES]


def from_heads(d):
    return [(j, i) for i, j in to_heads(d)]


OTHER_CORE = [(place(z, x, y, hi, c), place(z, x, y, hi, 1 - c)) for z, x, y, hi, c in DEVICES]
TO_FIRST = [(place(z, x, y, hi, 1), place(z, x, y, hi, 0)) for z, x, y, hi, c in DEVICES if c]
TO_SECOND = [(j, i) for i, j in TO_FIRST]
ALONG_Z = [
    (place(z, x, y, hi, c), place(z + 2 * c - 1, x, y, hi, c))
    for z, x, y, hi, c in DEVICES
    if 0 <= z + 2 * c - 1 < 4
]
BACK_Z = [(j, i) for i, j in ALONG_Z]
BACK_Z_SECOND = [(j, i) for j, i in BACK_Z if i % 2]


def nt(a, b):
    return lax.dot_general(a, b, (((1,), (1,)), ((), ())), preferred_element_type=F32)


def nn(a, b):
    return lax.dot_general(a, b, (((1,), (0,)), ((), ())), preferred_element_type=F32)


def tn(a, b):
    return lax.dot_general(a, b, (((0,), (0,)), ((), ())), preferred_element_type=F32)


def relay(moves, stage, sems):
    ins = [
        pltpu.make_async_copy(src, stage.at[n], sems.at[0, n]) for n, (src, _) in enumerate(moves)
    ]
    outs = [
        pltpu.make_async_copy(stage.at[n], dst, sems.at[1, n]) for n, (_, dst) in enumerate(moves)
    ]
    for copy in ins:
        copy.start()
    for n, copy in enumerate(ins):
        copy.wait()
        outs[n].start()
    for copy in outs:
        copy.wait()


def split_kernel(first_round, at, q, g, k, v, *refs):
    outs, (stage, sems) = refs[-6:-2], refs[-2:]
    y, x = at[0], at[1]
    for side, pair in ((0, (q, g)), (1, (k, v))):

        @pl.when(x == (side if first_round else 1 - side))
        def _(pair=pair):
            moves = []
            for d in range(4):
                lanes = pl.ds(pl.multiple_of(lax.rem(y + d, 4) * HEAD, HEAD), HEAD)
                moves += [(pair[n].at[:, lanes], outs[d].at[n]) for n in range(2)]
            relay(moves, stage, sems)


def gather_kernel(*refs):
    ins, out, stage, sems = refs[:4], *refs[4:]
    relay([(ins[d], out.at[:, pl.ds(3 * d, 3)]) for d in range(4)], stage, sems)


def pair_grads(scores, weight_grad, allowed):
    u = scores * U_SCALE
    t = jnp.tanh(u)
    p = jnp.where(allowed, 1.0 + t, 0.0)
    w = u * p
    slope = p + w * (1.0 - t)
    return w.astype(BF), (weight_grad * slope).astype(BF)


def pairs_kernel(phase, at, tab, cls, nvd, *refs):
    r1, r2 = refs[0:4], refs[4:8]
    extra = refs[8:10] if phase else refs[8:11]
    refs = refs[10:] if phase else refs[11:]
    if phase:
        dq_out, dk_out, dv_out = refs[:3]
        refs = refs[3:]
        qs, gs, ks, vs, dqa, dka, dva, s1, s2, sems = refs
    else:
        p1_out, p2_out, s1_out, s2_out, beside_out = refs[:5]
        qs, gs, ks, vs, dqa, dka, dva, sems = refs[5:]
    core, groups = at[2], at[3 + phase]
    low, high = pl.ds(0, HALF), pl.ds(HALF, HALF)

    def copies(own):
        qg, kv = ((r1, r2), (r2, r1))[own]
        out = []
        for d in range(4):
            rows = pl.ds(3 * d, 3)
            if phase == 1 or own == 1:
                out += [(qg[d].at[0], qs.at[rows]), (qg[d].at[1], gs.at[rows])]
            if phase == 1 or own == 0:
                out += [(kv[d].at[0], ks.at[rows]), (kv[d].at[1], vs.at[rows])]
        if phase == 0:
            across, beside = extra[0], extra[1 + own]
            out += [(beside.at[0], ks.at[high]), (beside.at[1], vs.at[high])]
            if own == 0:
                out += [(across.at[0], qs.at[low]), (across.at[1], gs.at[low])]
            else:
                out += [(across.at[0], ks.at[low]), (across.at[1], vs.at[low])]
        return [pltpu.make_async_copy(a, b, sems.at[i]) for i, (a, b) in enumerate(out)]

    def late():
        return [
            pltpu.make_async_copy(extra[0], s1, sems.at[20]),
            pltpu.make_async_copy(extra[1], s2, sems.at[21]),
        ]

    for own in range(2):

        @pl.when(core == own)
        def _(own=own):
            for copy in copies(own):
                copy.start()

    if phase:
        for copy in late():
            copy.start()
    dqa[...] = jnp.zeros_like(dqa)
    dka[...] = jnp.zeros_like(dka)
    dva[...] = jnp.zeros_like(dva)
    zero = jnp.zeros((BLK, HEAD), BF)
    dummy = DUMMY[phase]
    qs[HALF], gs[HALF], ks[dummy], vs[dummy] = zero, zero, zero, zero

    for own in range(2):

        @pl.when(core == own)
        def _(own=own):
            for copy in copies(own):
                copy.wait()

    def work(items, rows):
        made = []
        for q, k, mask in items:
            key, value, query, grad = ks[k, :rows], vs[k, :rows], qs[q], gs[q]
            made.append((q, k, mask, key, query, grad, nt(key, query), nt(value, grad)))
        for q, k, mask, key, query, grad, scores, weight_grad in made:
            w, sg = pair_grads(scores, weight_grad, mask)
            dva[k, :rows] += nn(w, grad)
            dka[k, :rows] += nn(sg, query)
            dqa[q] += tn(key, sg)

    def own_group(g, _):
        items = []
        row = lax.broadcasted_iota(jnp.int32, (BLK, BLK), 0)
        col = lax.broadcasted_iota(jnp.int32, (BLK, BLK), 1)
        for i in range(4):
            slot = g * 4 + i
            items.append((slot, slot, (row == col) | ((row < col) & (row < nvd[slot]))))
        work(items, BLK)
        return 0

    if phase:
        lax.fori_loop(0, 3, own_group, 0)

    def group(g, _):
        for c, rows in enumerate(CLASSES):

            @pl.when(cls[phase * LISTED + g] == c)
            def _(rows=rows):
                row = lax.broadcasted_iota(jnp.int32, (rows, BLK), 0)
                items = []
                for i in range(GROUP):
                    e = tab[phase * ENTRIES + g * GROUP + i]
                    items.append((e & 15, (e >> 4) & 31, row < ((e >> 9) & 511)))
                work(items, rows)

        return 0

    lax.fori_loop(0, groups, group, 0)

    if phase:
        for copy in late():
            copy.wait()

    def finish(s, _):
        dq, dk, dv = dqa[s].T * QK_SCALE, dka[s] * QK_SCALE, dva[s] * V_SCALE
        if phase:
            dq_out[s] = dq + jnp.where(core == 1, s1[s], 0.0)
            dk_out[s] = dk + jnp.where(core == 0, s1[s], 0.0)
            dv_out[s] = dv + jnp.where(core == 0, s2[s], 0.0)
        else:
            p1_out[s] = jnp.where(core == 0, dq, dk).astype(BF)
            p2_out[s] = dv.astype(BF)
            s1_out[s] = jnp.where(core == 0, dk, dq)
            s2_out[s] = dv
            beside_out[0, s] = (dka[HALF + s] * QK_SCALE).astype(BF)
            beside_out[1, s] = (dva[HALF + s] * V_SCALE).astype(BF)
        return 0

    lax.fori_loop(0, HALF, finish, 0)


def piped(ins, shapes, in_sems, outs, staged, out_sems, compute):
    def coming(d):
        rows = pl.ds(3 * d, 3)
        return [
            pltpu.make_async_copy(
                src.at[:, rows] if four else src.at[rows],
                dst.at[:, rows] if four else dst.at[rows],
                in_sems.at[d, n],
            )
            for n, (src, dst, four) in enumerate(zip(ins, shapes[0], shapes[1]))
        ]

    def going(d):
        return pltpu.make_async_copy(staged.at[d], outs[d], out_sems.at[d])

    for d in range(4):
        for copy in coming(d):
            copy.start()
    for d in range(4):
        for copy in coming(d):
            copy.wait()
        compute(d)
        going(d).start()
    for d in range(4):
        going(d).wait()


def dq_kernel(at, dq, across, o0, o1, o2, o3, dq_v, across_v, staged, in_sems, out_sems):
    first = at[2] == 0

    def compute(d):
        for m in range(3):
            s = 3 * d + m
            far = across_v[s].astype(F32)
            staged[d, m] = (dq_v[s] + jnp.where(first, far, 0.0)).astype(BF)

    piped(
        (dq, across), ((dq_v, across_v), (0, 0)), in_sems, (o0, o1, o2, o3), staged, out_sems, compute
    )


def dkv_kernel(at, *refs):
    ins, outs = refs[:5], refs[5:9]
    bufs, (staged, in_sems, out_sems) = refs[9:14], refs[14:]
    dk, dv, beside, a1, a2 = bufs
    first = at[2] == 0

    def compute(d):
        for m in range(3):
            s = 3 * d + m
            for n, (own, far) in enumerate(((dk, a1), (dv, a2))):
                near = beside[n, s].astype(F32)
                far = jnp.where(first, 0.0, far[s].astype(F32))
                staged[d, n, m] = (own[s] + near + far).astype(BF)

    piped(ins, (bufs, (0, 0, 1, 0, 0)), in_sems, outs, staged, out_sems, compute)


def join_kernel(arrays, at, *refs):
    outs, (stage, sems) = refs[4 : 4 + arrays], refs[-2:]
    moves = []
    for d in range(4):
        lanes = pl.ds(pl.multiple_of(lax.rem(at[0] + d, 4) * HEAD, HEAD), HEAD)
        moves += [(refs[d].at[n], outs[n].at[:, lanes]) for n in range(arrays)]
    relay(moves, stage, sems)


def call(kernel, outs, ins, scratch=(), limit=56, where=ANY, cost=None, **kw):
    return pl.pallas_call(
        kernel,
        out_shape=outs,
        in_specs=ins,
        out_specs=[where] * len(outs),
        scratch_shapes=scratch,
        compiler_params=pltpu.CompilerParams(vmem_limit_bytes=limit * 2**20),
        cost_estimate=cost,
        **kw,
    )


def table(qs, ks, valid, counts, dummy):
    rows = BLK - counts
    cls = jnp.clip((rows + 31) // 32 - 5, 0, 3)
    value = (qs | (ks << 4) | (rows << 9) | (cls << 18)).reshape(-1)
    order = jnp.where(valid, cls, 4).reshape(-1)
    n = jnp.arange(ENTRIES, dtype=jnp.int32)
    before = (order[None, :] < order[:, None]) | (
        (order[None, :] == order[:, None]) & (n[None, :] < n[:, None])
    )
    rank = jnp.sum(before.astype(jnp.int32), 1)
    total = jnp.sum(valid.astype(jnp.int32))
    tab = jnp.sum(jnp.where(rank[None, :] == n[:, None], value[None, :], 0), 1)
    tab = jnp.where(n < total, tab, HALF | (dummy << 4))
    return tab, jnp.max((tab >> 18).reshape(-1, GROUP), 1), (total + GROUP - 1) // GROUP


def tables(key_blocks, target_counts, z, y, core):
    def slot(t):
        return lax.rem(y + 4 - (t % HALF) // 3, 4) * 3 + t % 3

    ids = jnp.arange(96, dtype=jnp.int32)
    own = lax.dynamic_slice(key_blocks, (PLANE * z + HALF * core, 0), (HALF, KPB))[:, 1:]
    after = lax.dynamic_slice(key_blocks, (jnp.minimum(PLANE * (z + 1), 84), 0), (HALF, KPB))[:, 1:]
    qs = jnp.broadcast_to(slot(jnp.arange(HALF, dtype=jnp.int32))[:, None], own.shape)
    made = []
    for phase in range(2):
        kid = own if phase else jnp.where(core == 0, after, own)
        plane = jnp.maximum(kid, 0) // PLANE
        t = jnp.maximum(kid, 0) - PLANE * plane
        same = (plane == z) & (t // HALF == core)
        if phase:
            valid, ks = (kid >= 0) & same, slot(t)
        else:
            valid = (kid >= 0) & jnp.where(core == 0, (z < 3) & (plane == z), ~same)
            other = (plane == z) & (t // HALF != core)
            ks = slot(t) + jnp.where(other, HALF, 0)
        counts = jnp.sum(jnp.where(kid[..., None] == ids, target_counts, 0), -1)
        made.append(table(qs, ks, valid, counts, DUMMY[phase]))
    s = jnp.arange(HALF, dtype=jnp.int32)
    block = PLANE * z + HALF * core + lax.rem(y + 4 - s // 3, 4) * 3 + s % 3
    nvd = BLK - jnp.sum(jnp.where(block[:, None] == ids, target_counts, 0), -1)
    return made, nvd


def pairs_cost(pairs):
    return pl.CostEstimate(
        flops=pairs * 10 * BLK * BLK * HEAD, bytes_accessed=12 * 2**20, transcendentals=pairs * BLK * BLK
    )


def body(queries, keys, values, out_grad, key_blocks, target_counts):
    ctx, tp = lax.axis_index("ctx"), lax.axis_index("tp")
    z, x, y, core = ctx // 8, (ctx // 4) % 2, ctx % 4, tp % 2
    here = jnp.stack([y, x]).astype(jnp.int32)
    rows = queries.shape[0]
    shape = jax.ShapeDtypeStruct
    dma = lambda *n: pltpu.SemaphoreType.DMA(n)

    def split(first_round, *behind):
        return call(
            functools.partial(split_kernel, first_round),
            [shape((2, rows, HEAD), BF)] * 4,
            [SMEM] + [ANY] * (4 + len(behind)),
            [pltpu.VMEM((8, rows, HEAD), BF), dma(2, 8)],
            limit=56,
            name="split",
        )(here, queries, out_grad, keys, values, *behind)

    def send(pieces, pairs):
        return [lax.ppermute(p, AXES, pairs(d)) for d, p in enumerate(pieces)]

    two = shape((2, HALF, BLK, HEAD), BF)

    stage = pltpu.VMEM((4, 2, 3, BLK, HEAD), BF)

    def gather(pieces):
        return call(gather_kernel, [two], [ANY] * 4, [stage, dma(2, 4)], limit=56, name="gather")(*pieces)[0]

    def blocks(pieces):
        return [p.reshape(2, 3, BLK, HEAD) for p in pieces]

    sent1 = split(True)
    sent2 = split(False, sent1[0])
    r1 = blocks(send(sent1, to_heads))
    r2 = blocks(send(sent2, to_heads))
    all1 = gather(r1)
    across = lax.ppermute(all1, AXES, ALONG_Z)
    to_first = lax.ppermute(all1, AXES, TO_FIRST)
    to_second = lax.ppermute(gather(r2), AXES, TO_SECOND)

    (far, own), nvd = tables(key_blocks, target_counts, z, y, core)
    at = jnp.stack([y, x, core, far[2], own[2]]).astype(jnp.int32)
    tab = jnp.concatenate([far[0], own[0]])
    cls = jnp.concatenate([far[1], own[1]])
    half, half16 = shape((HALF, BLK, HEAD), F32), shape((HALF, BLK, HEAD), BF)

    def scratch(k):
        return [
            pltpu.VMEM((HALF + 1, BLK, HEAD), BF),
            pltpu.VMEM((HALF + 1, BLK, HEAD), BF),
            pltpu.VMEM((k + 1, BLK, HEAD), BF),
            pltpu.VMEM((k + 1, BLK, HEAD), BF),
            pltpu.VMEM((HALF + 1, HEAD, BLK), F32),
            pltpu.VMEM((k + 1, BLK, HEAD), F32),
            pltpu.VMEM((k + 1, BLK, HEAD), F32),
        ]

    p1, p2, s1, s2, beside = call(
        functools.partial(pairs_kernel, 0),
        [half16, half16, half, half, two],
        [SMEM] * 4 + [ANY] * 11,
        scratch(PLANE) + [dma(22)],
        where=VMEM,
        cost=pairs_cost(139),
        name="far",
    )(at, tab, cls, nvd, *r1, *r2, across, to_first, to_second)
    p1 = lax.ppermute(p1, AXES, BACK_Z)
    p2 = lax.ppermute(p2, AXES, BACK_Z_SECOND)
    beside = lax.ppermute(beside, AXES, OTHER_CORE)
    dq, dk, dv = call(
        functools.partial(pairs_kernel, 1),
        [half, half, half],
        [SMEM] * 4 + [ANY] * 10,
        scratch(HALF) + [pltpu.VMEM((HALF, BLK, HEAD), F32)] * 2 + [dma(22)],
        where=VMEM,
        cost=pairs_cost(60),
        name="own",
    )(at, tab, cls, nvd, *r1, *r2, s1, s2)
    v3, v3h = pltpu.VMEM((HALF, BLK, HEAD), F32), pltpu.VMEM((HALF, BLK, HEAD), BF)
    v4 = pltpu.VMEM((2, HALF, BLK, HEAD), BF)
    dq_sent = call(
        dq_kernel,
        [shape((3, BLK, HEAD), BF)] * 4,
        [SMEM] + [ANY] * 2,
        [v3, v3h, pltpu.VMEM((4, 3, BLK, HEAD), BF), dma(4, 2), dma(4)],
        name="dq",
    )(at, dq, p1)
    dq_back = send([p.reshape(1, rows, HEAD) for p in dq_sent], from_heads)
    dkv_sent = call(
        dkv_kernel,
        [shape((2, 3, BLK, HEAD), BF)] * 4,
        [SMEM] + [ANY] * 5,
        [v3, v3, v4, v3h, v3h, pltpu.VMEM((4, 2, 3, BLK, HEAD), BF), dma(4, 5), dma(4)],
        name="dkv",
    )(at, dk, dv, beside, p1, p2)
    dkv_back = send([p.reshape(2, rows, HEAD) for p in dkv_sent], from_heads)
    out = shape(queries.shape, BF)

    def join(pieces, arrays):
        return call(
            functools.partial(join_kernel, arrays),
            [out] * arrays,
            [SMEM] + [ANY] * 4,
            [pltpu.VMEM((4 * arrays, rows, HEAD), BF), dma(2, 4 * arrays)],
            limit=56,
            name="join",
        )(here, *pieces)

    return (*join(dq_back, 1), *join(dkv_back, 2))


def solution(mesh):
    in_specs = (P("ctx", "tp"),) * 4 + (P(), P())
    return jax.shard_map(
        body, mesh=mesh, in_specs=in_specs, out_specs=(P("ctx", "tp"),) * 3, check_vma=False
    )
```

```python
import functools
import math

import jax
import jax.numpy as jnp
from jax import lax
from jax.experimental import pallas as pl
from jax.experimental.pallas import tpu as pltpu
from jax.sharding import PartitionSpec as P

F32, BF = jnp.float32, jnp.bfloat16
HEAD, BLK, KPB = 128, 256, 16
PLANE, HALF = 24, 12
AXES = ("ctx", "tp")
U_SCALE = 0.5 / math.sqrt(HEAD)
V_SCALE = 1.0 / math.sqrt(KPB * BLK)
QK_SCALE = 0.5 * V_SCALE / math.sqrt(HEAD)
GROUP = 6
CLASSES = (160, 192, 224, 256)
SPOTS = 256
MOST = 10
DUMMY = (24, 12)
VMEM = pl.BlockSpec(memory_space=pltpu.VMEM)
SMEM = pl.BlockSpec(memory_space=pltpu.SMEM)
ANY = pl.BlockSpec(memory_space=pl.ANY)


def place(z, x, y, hi, core):
    return (z * 8 + x * 4 + y % 4) * 4 + hi * 2 + core


DEVICES = [
    (z, x, y, hi, core)
    for z in range(4)
    for x in range(2)
    for y in range(4)
    for hi in range(2)
    for core in range(2)
]


def to_heads(d):
    return [(place(z, x, y, hi, c), place(z, c, y + d, hi, x)) for z, x, y, hi, c in DEVICES]


def from_heads(d):
    return [(j, i) for i, j in to_heads(d)]


OTHER_CORE = [(place(z, x, y, hi, c), place(z, x, y, hi, 1 - c)) for z, x, y, hi, c in DEVICES]
ALONG_Z = [
    (place(z, x, y, hi, c), place(z + 2 * c - 1, x, y, hi, c))
    for z, x, y, hi, c in DEVICES
    if 0 <= z + 2 * c - 1 < 4
]
BACK_Z = [(j, i) for i, j in ALONG_Z]
BACK_Z_SECOND = [(j, i) for j, i in BACK_Z if i % 2]


def nt(a, b):
    return lax.dot_general(a, b, (((1,), (1,)), ((), ())), preferred_element_type=F32)


def nn(a, b):
    return lax.dot_general(a, b, (((1,), (0,)), ((), ())), preferred_element_type=F32)


def tn(a, b):
    return lax.dot_general(a, b, (((0,), (0,)), ((), ())), preferred_element_type=F32)


def relay(moves, stage, sems):
    ins = [
        pltpu.make_async_copy(src, stage.at[n], sems.at[0, n]) for n, (src, _) in enumerate(moves)
    ]
    outs = [
        pltpu.make_async_copy(stage.at[n], dst, sems.at[1, n]) for n, (_, dst) in enumerate(moves)
    ]
    for copy in ins:
        copy.start()
    for n, copy in enumerate(ins):
        copy.wait()
        outs[n].start()
    for copy in outs:
        copy.wait()


def split_kernel(first_round, at, q, g, k, v, *refs):
    outs, (stage, sems) = refs[-6:-2], refs[-2:]
    y, x = at[0], at[1]
    for side, pair in ((0, (q, g)), (1, (k, v))):

        @pl.when(x == (side if first_round else 1 - side))
        def _(pair=pair):
            moves = []
            for d in range(4):
                lanes = pl.ds(pl.multiple_of(lax.rem(y + d, 4) * HEAD, HEAD), HEAD)
                moves += [(pair[n].at[:, lanes], outs[d].at[n]) for n in range(2)]
            relay(moves, stage, sems)


def gather_kernel(*refs):
    ins, (out, stage, sems) = refs[:4], refs[-3:]
    relay([(ins[d], out.at[:, pl.ds(3 * d, 3)]) for d in range(4)], stage, sems)


def gather_keys_kernel(at, *refs):
    ins, (most, rest, stage, sems) = refs[:8], refs[8:]
    for own, pieces in ((0, ins[4:]), (1, ins[:4])):

        @pl.when(at[2] == own)
        def _(pieces=pieces):
            moves = []
            for d in range(4):
                for m in range(3):
                    b = 3 * d + m
                    to = most.at[:, b] if b < MOST else rest.at[:, b - MOST]
                    moves.append((pieces[d].at[:, m], to))
            relay(moves, stage, sems)


def pair_grads(scores, weight_grad, allowed):
    u = scores * U_SCALE
    t = jnp.tanh(u)
    p = jnp.where(allowed, 1.0 + t, 0.0)
    w = u * p
    slope = p + w * (1.0 - t)
    return w.astype(BF), (weight_grad * slope).astype(BF)


def pairs_kernel(phase, at, tab, *refs):
    r1, r2 = refs[0:4], refs[4:8]
    extra = refs[8:10] if phase else refs[8:11]
    refs = refs[10:] if phase else refs[11:]
    if phase:
        outs, refs = refs[:3], refs[3:]
        (*made, s1, s2), refs = refs[:5], refs[5:]
    else:
        outs, refs = refs[:4], refs[4:]
        made, refs = refs[:5], refs[5:]
    qs, gs, ks, vs, dqa, dka, dva, sems = refs
    core, groups = at[2], (tab[phase, SPOTS - 1] + GROUP - 1) // GROUP

    def copies(own):
        qg, kv = ((r1, r2), (r2, r1))[own]
        out = []
        for d in range(4):
            rows = pl.ds(3 * d, 3)
            if phase == 1 or own == 1:
                out += [(qg[d].at[0], qs.at[rows]), (qg[d].at[1], gs.at[rows])]
            if phase == 1 or own == 0:
                out += [(kv[d].at[0], ks.at[rows]), (kv[d].at[1], vs.at[rows])]
        if phase == 0:
            across, most, rest = extra
            to = (ks, vs) if own else (qs, gs)
            for n in range(2):
                out.append((across.at[n], to[n].at[pl.ds(0, HALF)]))
                out.append((most.at[n], (ks, vs)[n].at[pl.ds(HALF, MOST)]))
                out.append((rest.at[n], (ks, vs)[n].at[pl.ds(HALF + MOST, HALF - MOST)]))
        return [pltpu.make_async_copy(a, b, sems.at[i]) for i, (a, b) in enumerate(out)]

    def late():
        return [
            pltpu.make_async_copy(extra[0], s1, sems.at[42]),
            pltpu.make_async_copy(extra[1], s2, sems.at[43]),
        ]

    for own in range(2):

        @pl.when(core == own)
        def _(own=own):
            for copy in copies(own):
                copy.start()

    if phase:
        for copy in late():
            copy.start()
    dqa[...] = jnp.zeros_like(dqa)
    dka[...] = jnp.zeros_like(dka)
    dva[...] = jnp.zeros_like(dva)
    zero = jnp.zeros((BLK, HEAD), BF)
    dummy = DUMMY[phase]
    qs[HALF], gs[HALF], ks[dummy], vs[dummy] = zero, zero, zero, zero

    for own in range(2):

        @pl.when(core == own)
        def _(own=own):
            for copy in copies(own):
                copy.wait()

    def work(items, rows):
        made = []
        for q, k, mask in items:
            key, value, query, grad = ks[k, :rows], vs[k, :rows], qs[q], gs[q]
            made.append((q, k, mask, key, query, grad, nt(key, query), nt(value, grad)))
        for q, k, mask, key, query, grad, scores, weight_grad in made:
            w, sg = pair_grads(scores, weight_grad, mask)
            dva[k, :rows] += nn(w, grad)
            dka[k, :rows] += nn(sg, query)
            dqa[q] += tn(key, sg)

    def own_group(g, _):
        items = []
        row = lax.broadcasted_iota(jnp.int32, (BLK, BLK), 0)
        col = lax.broadcasted_iota(jnp.int32, (BLK, BLK), 1)
        for i in range(4):
            slot = g * 4 + i
            items.append((slot, slot, (row == col) | ((row < col) & (row < tab[2, slot]))))
        work(items, BLK)
        return 0

    if phase:
        lax.fori_loop(0, 3, own_group, 0)

    def group(g, _):
        for c, rows in enumerate(CLASSES):

            @pl.when((tab[phase, g * GROUP + GROUP - 1] >> 18) == c)
            def _(rows=rows):
                row = lax.broadcasted_iota(jnp.int32, (rows, BLK), 0)
                items = []
                for i in range(GROUP):
                    e = tab[phase, g * GROUP + i]
                    items.append((e & 15, (e >> 4) & 31, row < ((e >> 9) & 511)))
                work(items, rows)

        return 0

    lax.fori_loop(0, groups, group, 0)

    if phase:
        for copy in late():
            copy.wait()

    def finish(s):
        dq, dk, dv = dqa[s].T * QK_SCALE, dka[s] * QK_SCALE, dva[s] * V_SCALE
        if phase:
            before, last = s1[s].astype(F32), s2[s].astype(F32)
            made[0][s] = (dq + jnp.where(core == 1, before, 0.0)).astype(BF)
            made[1][s] = (dk + jnp.where(core == 0, before, 0.0)).astype(BF)
            made[2][s] = (dv + jnp.where(core == 0, last, 0.0)).astype(BF)
        else:
            made[0][s] = jnp.where(core == 0, dq, dk).astype(BF)
            made[1][s] = dv.astype(BF)
            made[2][s] = jnp.where(core == 0, dk, dq).astype(BF)
            made[3][s] = (dka[HALF + s] * QK_SCALE).astype(BF)
            made[4][s] = (dva[HALF + s] * V_SCALE).astype(BF)

    targets = outs if phase else (outs[0], outs[1], outs[2], outs[3].at[0], outs[3].at[1])
    going = []
    for part in range(4):
        lax.fori_loop(3 * part, 3 * part + 3, lambda s, _: (finish(s), 0)[1], 0)
        rows = pl.ds(3 * part, 3)
        for n, (src, dst) in enumerate(zip(made, targets)):
            going.append(
                pltpu.make_async_copy(src.at[rows], dst.at[rows], sems.at[5 * part + n])
            )
            going[-1].start()
    for copy in going:
        copy.wait()


def piped(ins, shapes, in_sems, outs, staged, out_sems, compute):
    def coming(d):
        rows = pl.ds(3 * d, 3)
        return [
            pltpu.make_async_copy(
                src.at[:, rows] if four else src.at[rows],
                dst.at[:, rows] if four else dst.at[rows],
                in_sems.at[d, n],
            )
            for n, (src, dst, four) in enumerate(zip(ins, shapes[0], shapes[1]))
        ]

    def going(d):
        return pltpu.make_async_copy(staged.at[d], outs[d], out_sems.at[d])

    for d in range(4):
        for copy in coming(d):
            copy.start()
    for d in range(4):
        for copy in coming(d):
            copy.wait()
        compute(d)
        going(d).start()
    for d in range(4):
        going(d).wait()


def sum_kernel(at, *refs):
    ins, outs = refs[:6], refs[6:10]
    bufs, (staged, in_sems, out_sems) = refs[10:16], refs[16:]
    dq, dk, dv, beside, a1, a2 = bufs
    first = at[2] == 0

    def compute(d):
        for m in range(3):
            s = 3 * d + m
            far = a1[s].astype(F32)
            last = jnp.where(first, 0.0, a2[s].astype(F32))
            staged[d, 0, m] = (dq[s].astype(F32) + jnp.where(first, far, 0.0)).astype(BF)
            far = jnp.where(first, 0.0, far)
            staged[d, 1, m] = (dk[s].astype(F32) + beside[0, s].astype(F32) + far).astype(BF)
            staged[d, 2, m] = (dv[s].astype(F32) + beside[1, s].astype(F32) + last).astype(BF)

    piped(ins, (bufs, (0, 0, 0, 1, 0, 0)), in_sems, outs, staged, out_sems, compute)


def join_kernel(arrays, at, *refs):
    outs, (stage, sems) = refs[4 : 4 + arrays], refs[-2:]
    moves = []
    for d in range(4):
        lanes = pl.ds(pl.multiple_of(lax.rem(at[0] + d, 4) * HEAD, HEAD), HEAD)
        moves += [(refs[d].at[n], outs[n].at[:, lanes]) for n in range(arrays)]
    relay(moves, stage, sems)


def call(kernel, outs, ins, scratch=(), limit=56, where=ANY, cost=None, **kw):
    return pl.pallas_call(
        kernel,
        out_shape=outs,
        in_specs=ins,
        out_specs=[where] * len(outs),
        scratch_shapes=scratch,
        compiler_params=pltpu.CompilerParams(vmem_limit_bytes=limit * 2**20),
        cost_estimate=cost,
        **kw,
    )


def table_kernel(at, counts, rows, out):
    y, core, z = at[0], at[2], at[3]
    shape = rows.shape[1:]
    lane = lax.broadcasted_iota(jnp.int32, shape, 1)
    line = lax.broadcasted_iota(jnp.int32, shape, 0)
    spot = lax.broadcasted_iota(jnp.int32, (shape[0], SPOTS), 1)
    ahead = (
        lax.broadcasted_iota(jnp.int32, (128, 128), 0)
        < lax.broadcasted_iota(jnp.int32, (128, 128), 1)
    ).astype(F32)
    above = (
        lax.broadcasted_iota(jnp.int32, (shape[0], shape[0]), 1)
        < lax.broadcasted_iota(jnp.int32, (shape[0], shape[0]), 0)
    ).astype(F32)

    def at_least(a, *bounds):
        return sum((a >= b).astype(jnp.int32) for b in bounds)

    def slot(u):
        third = at_least(u, 3, 6, 9)
        return ((y - third) & 3) * 3 + u - 3 * third

    def place_values(rank, value, columns):
        made = jnp.zeros((shape[0], SPOTS), jnp.int32)
        for j in columns:
            made += jnp.where(rank[:, j : j + 1] == spot, value[:, j : j + 1], 0)
        return jnp.sum(made, 0, keepdims=True)

    for phase in range(2):
        kid = rows[0] if phase else jnp.where(core == 0, rows[1], rows[0])
        kept = jnp.zeros(shape, jnp.int32)
        for k in range(4 * PLANE):
            kept = jnp.where(kid == k, BLK - counts[k], kept)
        plane = at_least(kid, PLANE, 2 * PLANE, 3 * PLANE)
        t = kid - PLANE * plane
        half = at_least(t, HALF)
        listed = (
            at_least(kid, 0) * at_least(lane, 1) * (1 - at_least(lane, KPB)) * (1 - at_least(line, HALF))
        )
        here, same = (plane == z).astype(jnp.int32), (half == core).astype(jnp.int32)
        ks = slot(t - HALF * half)
        if phase:
            valid = listed * here * same
        else:
            above_it = (z < 3).astype(jnp.int32)
            valid = listed * jnp.where(core == 0, here * above_it, 1 - here * same)
            ks = ks + HALF * here * (1 - same)
        cls = jnp.clip(((kept + 31) >> 5) - 5, 0, 3)
        value = slot(line) | (ks << 4) | (kept << 9) | (cls << 18)
        rank, total = jnp.full(shape, -1, jnp.int32), 0
        for c in range(4):
            mine = valid * (cls == c).astype(jnp.int32)
            ones = mine.astype(F32)
            before = nn(ones, ahead) + jnp.sum(nn(above, ones), 1, keepdims=True)
            rank = jnp.where(mine > 0, total + before.astype(jnp.int32), rank)
            total = total + jnp.sum(mine)
        made = place_values(rank, value, range(1, KPB))
        first = spot[:1]
        made = jnp.where(first < total, made, HALF | (DUMMY[phase] << 4) | (3 << 18))
        out[phase : phase + 1] = jnp.where(first == SPOTS - 1, total, made)
        if phase:
            out[2:3] = place_values(jnp.where(line < HALF, slot(line), -1), kept, (0,))


def pairs_cost(pairs):
    return pl.CostEstimate(
        flops=pairs * 10 * BLK * BLK * HEAD, bytes_accessed=12 * 2**20, transcendentals=pairs * BLK * BLK
    )


def body(queries, keys, values, out_grad, key_blocks, target_counts):
    ctx, tp = lax.axis_index("ctx"), lax.axis_index("tp")
    z, x, y, core = ctx // 8, (ctx // 4) % 2, ctx % 4, tp % 2
    at = jnp.stack([y, x, core, z]).astype(jnp.int32)
    rows = queries.shape[0]
    shape = jax.ShapeDtypeStruct
    dma = lambda *n: pltpu.SemaphoreType.DMA(n)
    own = lax.dynamic_slice(key_blocks, (PLANE * z + HALF * core, 0), (HALF, KPB))
    after = lax.dynamic_slice(key_blocks, (jnp.minimum(PLANE * (z + 1), 84), 0), (HALF, KPB))
    lists = jnp.pad(jnp.stack([own, after]), ((0, 0), (0, 4), (0, 128 - KPB)), constant_values=-1)
    tab = call(
        table_kernel,
        [shape((3, SPOTS), jnp.int32)],
        [SMEM, SMEM, VMEM],
        where=VMEM,
        name="table",
    )(at, target_counts, lists)[0]
    half = shape((HALF, BLK, HEAD), BF)

    def split(first_round, *behind):
        return call(
            functools.partial(split_kernel, first_round),
            [shape((2, rows, HEAD), BF)] * 4,
            [SMEM] + [ANY] * (4 + len(behind)),
            [pltpu.VMEM((8, rows, HEAD), BF), dma(2, 8)],
            limit=56,
            name="split",
        )(at, queries, out_grad, keys, values, *behind)

    def send(pieces, pairs):
        return [lax.ppermute(p, AXES, pairs(d)) for d, p in enumerate(pieces)]

    two = shape((2, HALF, BLK, HEAD), BF)


    def blocks(pieces):
        return [p.reshape(2, 3, BLK, HEAD) for p in pieces]

    sent1 = split(True)
    sent2 = split(False, sent1[0], tab)
    r1 = blocks(send(sent1, to_heads))
    r2 = blocks(send(sent2, to_heads))
    first = call(
        gather_kernel,
        [two],
        [ANY] * 5,
        [pltpu.VMEM((4, 2, 3, BLK, HEAD), BF), dma(2, 4)],
        name="gather",
    )(*r1, sent2[0])[0]
    across = lax.ppermute(first, AXES, ALONG_Z)
    near = call(
        gather_keys_kernel,
        [shape((2, n, BLK, HEAD), BF) for n in (MOST, HALF - MOST)],
        [SMEM] + [ANY] * 8,
        [pltpu.VMEM((HALF, 2, BLK, HEAD), BF), dma(2, HALF)],
        name="gather_keys",
    )(at, *r1, *r2)
    near = [lax.ppermute(n, AXES, OTHER_CORE) for n in near]

    def scratch(k):
        return [
            pltpu.VMEM((HALF + 1, BLK, HEAD), BF),
            pltpu.VMEM((HALF + 1, BLK, HEAD), BF),
            pltpu.VMEM((k + 1, BLK, HEAD), BF),
            pltpu.VMEM((k + 1, BLK, HEAD), BF),
            pltpu.VMEM((HALF + 1, HEAD, BLK), F32),
            pltpu.VMEM((k + 1, BLK, HEAD), F32),
            pltpu.VMEM((k + 1, BLK, HEAD), F32),
        ]

    parts = [pltpu.VMEM((HALF, BLK, HEAD), BF)] * 5
    p1, p2, s1, beside = call(
        functools.partial(pairs_kernel, 0),
        [half, half, half, two],
        [SMEM] * 2 + [ANY] * 11,
        parts + scratch(PLANE) + [dma(44)],
        cost=pairs_cost(139),
        name="far",
    )(at, tab, *r1, *r2, across, *near)
    s2 = p2
    p1 = lax.ppermute(p1, AXES, BACK_Z)
    p2 = lax.ppermute(p2, AXES, BACK_Z_SECOND)
    beside = lax.ppermute(beside, AXES, OTHER_CORE)
    dq, dk, dv = call(
        functools.partial(pairs_kernel, 1),
        [half, half, half],
        [SMEM] * 2 + [ANY] * 10,
        parts + scratch(HALF) + [dma(44)],
        cost=pairs_cost(60),
        name="own",
    )(at, tab, *r1, *r2, s1, s2)
    v3, v4 = pltpu.VMEM((HALF, BLK, HEAD), BF), pltpu.VMEM((2, HALF, BLK, HEAD), BF)
    sums = call(
        sum_kernel,
        [shape((3, 3, BLK, HEAD), BF)] * 4,
        [SMEM] + [ANY] * 6,
        [v3, v3, v3, v4, v3, v3, pltpu.VMEM((4, 3, 3, BLK, HEAD), BF), dma(4, 6), dma(4)],
        name="sums",
    )(at, dq, dk, dv, beside, p1, p2)
    back = send([p.reshape(3, rows, HEAD) for p in sums], from_heads)
    out = shape(queries.shape, BF)
    return tuple(
        call(
            functools.partial(join_kernel, 3),
            [out] * 3,
            [SMEM] + [ANY] * 4,
            [pltpu.VMEM((12, rows, HEAD), BF), dma(2, 12)],
            name="join",
        )(at, *back)
    )


def solution(mesh):
    in_specs = (P("ctx", "tp"),) * 4 + (P(), P())
    return jax.shard_map(
        body, mesh=mesh, in_specs=in_specs, out_specs=(P("ctx", "tp"),) * 3, check_vma=False
    )
```

```python
import functools
import math

import jax
import jax.numpy as jnp
from jax import lax
from jax.experimental import pallas as pl
from jax.experimental.pallas import tpu as pltpu
from jax.sharding import PartitionSpec as P

F32, BF = jnp.float32, jnp.bfloat16
HEAD, BLK, KPB = 128, 256, 16
PLANE, HALF = 24, 12
AXES = ("ctx", "tp")
U_SCALE = 0.5 / math.sqrt(HEAD)
V_SCALE = 1.0 / math.sqrt(KPB * BLK)
QK_SCALE = 0.5 * V_SCALE / math.sqrt(HEAD)
GROUP = (8, 6)
CLASSES = (160, 192, 224, 256)
SPOTS = 256
MOST = 10
DUMMY = (24, 12)
VMEM = pl.BlockSpec(memory_space=pltpu.VMEM)
SMEM = pl.BlockSpec(memory_space=pltpu.SMEM)
ANY = pl.BlockSpec(memory_space=pl.ANY)


def place(z, x, y, hi, core):
    return (z * 8 + x * 4 + y % 4) * 4 + hi * 2 + core


DEVICES = [
    (z, x, y, hi, core)
    for z in range(4)
    for x in range(2)
    for y in range(4)
    for hi in range(2)
    for core in range(2)
]


def to_heads(d):
    return [(place(z, x, y, hi, c), place(z, c, y + d, hi, x)) for z, x, y, hi, c in DEVICES]


def from_heads(d):
    return [(j, i) for i, j in to_heads(d)]


OTHER_CORE = [(place(z, x, y, hi, c), place(z, x, y, hi, 1 - c)) for z, x, y, hi, c in DEVICES]
ALONG_Z = [
    (place(z, x, y, hi, c), place(z + 2 * c - 1, x, y, hi, c))
    for z, x, y, hi, c in DEVICES
    if 0 <= z + 2 * c - 1 < 4
]
BACK_Z = [(j, i) for i, j in ALONG_Z]
BACK_Z_SECOND = [(j, i) for j, i in BACK_Z if i % 2]


def nt(a, b):
    return lax.dot_general(a, b, (((1,), (1,)), ((), ())), preferred_element_type=F32)


def nn(a, b):
    return lax.dot_general(a, b, (((1,), (0,)), ((), ())), preferred_element_type=F32)


def tn(a, b):
    return lax.dot_general(a, b, (((0,), (0,)), ((), ())), preferred_element_type=F32)


def relay(moves, stage, sems):
    ins = [
        pltpu.make_async_copy(src, stage.at[n], sems.at[0, n]) for n, (src, _) in enumerate(moves)
    ]
    outs = [
        pltpu.make_async_copy(stage.at[n], dst, sems.at[1, n]) for n, (_, dst) in enumerate(moves)
    ]
    for copy in ins:
        copy.start()
    for n, copy in enumerate(ins):
        copy.wait()
        outs[n].start()
    for copy in outs:
        copy.wait()


def split_kernel(first_round, at, q, g, k, v, *refs):
    outs, (stage, sems) = refs[-6:-2], refs[-2:]
    y, x = at[0], at[1]
    for side, pair in ((0, (q, g)), (1, (k, v))):

        @pl.when(x == (side if first_round else 1 - side))
        def _(pair=pair):
            moves = []
            for d in range(4):
                lanes = pl.ds(pl.multiple_of(lax.rem(y + d, 4) * HEAD, HEAD), HEAD)
                moves += [(pair[n].at[:, lanes], outs[d].at[n]) for n in range(2)]
            relay(moves, stage, sems)


def gather_kernel(*refs):
    ins, (out, stage, sems) = refs[:4], refs[-3:]
    relay([(ins[d], out.at[:, pl.ds(3 * d, 3)]) for d in range(4)], stage, sems)


def gather_keys_kernel(at, *refs):
    ins, (most, rest, stage, sems) = refs[:8], refs[8:]
    for own, pieces in ((0, ins[4:]), (1, ins[:4])):

        @pl.when(at[2] == own)
        def _(pieces=pieces):
            moves = []
            for d in range(4):
                for m in range(3):
                    b = 3 * d + m
                    to = most.at[:, b] if b < MOST else rest.at[:, b - MOST]
                    moves.append((pieces[d].at[:, m], to))
            relay(moves, stage, sems)


def pair_grads(scores, weight_grad, allowed):
    u = scores * U_SCALE
    t = jnp.tanh(u)
    p = 1.0 + t
    if allowed is not None:
        p = jnp.where(allowed, p, 0.0)
    w = u * p
    slope = p + w * (1.0 - t)
    return w.astype(BF), (weight_grad * slope).astype(BF)


def pairs_kernel(phase, at, tab, *refs):
    r1, r2 = refs[0:4], refs[4:8]
    extra = refs[8:10] if phase else refs[8:11]
    refs = refs[10:] if phase else refs[11:]
    if phase:
        outs, refs = refs[:3], refs[3:]
        (*made, s1, s2), refs = refs[:5], refs[5:]
    else:
        outs, refs = refs[:4], refs[4:]
        made, refs = refs[:5], refs[5:]
    qs, gs, ks, vs, dqa, dka, dva, sems = refs
    core, size = at[2], GROUP[phase]
    groups = (tab[phase, SPOTS - 1] + size - 1) // size

    def copies(own):
        qg, kv = ((r1, r2), (r2, r1))[own]
        out = []
        for d in range(4):
            rows = pl.ds(3 * d, 3)
            if phase == 1 or own == 1:
                out += [(qg[d].at[0], qs.at[rows]), (qg[d].at[1], gs.at[rows])]
            if phase == 1 or own == 0:
                out += [(kv[d].at[0], ks.at[rows]), (kv[d].at[1], vs.at[rows])]
        if phase == 0:
            across, most, rest = extra
            to = (ks, vs) if own else (qs, gs)
            for n in range(2):
                out.append((across.at[n], to[n].at[pl.ds(0, HALF)]))
                out.append((most.at[n], (ks, vs)[n].at[pl.ds(HALF, MOST)]))
                out.append((rest.at[n], (ks, vs)[n].at[pl.ds(HALF + MOST, HALF - MOST)]))
        return [pltpu.make_async_copy(a, b, sems.at[i]) for i, (a, b) in enumerate(out)]

    def late():
        return [
            pltpu.make_async_copy(extra[0], s1, sems.at[42]),
            pltpu.make_async_copy(extra[1], s2, sems.at[43]),
        ]

    for own in range(2):

        @pl.when(core == own)
        def _(own=own):
            for copy in copies(own):
                copy.start()

    if phase:
        for copy in late():
            copy.start()
    dqa[...] = jnp.zeros_like(dqa)
    dka[...] = jnp.zeros_like(dka)
    dva[...] = jnp.zeros_like(dva)
    zero = jnp.zeros((BLK, HEAD), BF)
    dummy = DUMMY[phase]
    qs[HALF], gs[HALF], ks[dummy], vs[dummy] = zero, zero, zero, zero

    for own in range(2):

        @pl.when(core == own)
        def _(own=own):
            for copy in copies(own):
                copy.wait()

    def work(items, rows):
        def scores(item):
            q, k, mask = item
            key, value, query, grad = ks[k, :rows], vs[k, :rows], qs[q], gs[q]
            return q, k, mask, key, query, grad, nt(key, query), nt(value, grad)

        def grads(q, k, mask, key, query, grad, score, weight_grad):
            made = [
                pair_grads(score[lo:hi], weight_grad[lo:hi], mask(lo, hi))
                for lo, hi in ((0, 128), (128, rows))
            ]
            w, sg = (jnp.concatenate(parts) for parts in zip(*made))
            dva[k, :rows] += nn(w, grad)
            dka[k, :rows] += nn(sg, query)
            dqa[q] += tn(key, sg)

        ahead = scores(items[0])
        for item in (*items[1:], None):
            now, ahead = ahead, None if item is None else scores(item)
            grads(*now)

    def own_group(g, _):
        def mask_of(slot):
            def mask(lo, hi):
                row = lo + lax.broadcasted_iota(jnp.int32, (hi - lo, BLK), 0)
                col = lax.broadcasted_iota(jnp.int32, (hi - lo, BLK), 1)
                return (row == col) | ((row < col) & (row < tab[2, slot]))

            return mask

        slots = [g * 6 + i for i in range(6)]
        work([(slot, slot, mask_of(slot)) for slot in slots], BLK)
        return 0

    if phase:
        lax.fori_loop(0, 2, own_group, 0)

    def mask_from(kept):
        def mask(lo, hi):
            if lo == 0:
                return None
            return lo + lax.broadcasted_iota(jnp.int32, (hi - lo, BLK), 0) < kept

        return mask

    def group(g, _):
        for c, rows in enumerate(CLASSES):

            @pl.when((tab[phase, g * size + size - 1] >> 18) == c)
            def _(rows=rows):
                items = []
                for i in range(size):
                    e = tab[phase, g * size + i]
                    items.append((e & 15, (e >> 4) & 31, mask_from((e >> 9) & 511)))
                work(items, rows)

        return 0

    lax.fori_loop(0, groups, group, 0)

    if phase:
        for copy in late():
            copy.wait()

    def finish(s):
        dq, dk, dv = dqa[s].T * QK_SCALE, dka[s] * QK_SCALE, dva[s] * V_SCALE
        if phase:
            before, last = s1[s].astype(F32), s2[s].astype(F32)
            made[0][s] = (dq + jnp.where(core == 1, before, 0.0)).astype(BF)
            made[1][s] = (dk + jnp.where(core == 0, before, 0.0)).astype(BF)
            made[2][s] = (dv + jnp.where(core == 0, last, 0.0)).astype(BF)
        else:
            made[0][s] = jnp.where(core == 0, dq, dk).astype(BF)
            made[1][s] = dv.astype(BF)
            made[2][s] = jnp.where(core == 0, dk, dq).astype(BF)
            made[3][s] = (dka[HALF + s] * QK_SCALE).astype(BF)
            made[4][s] = (dva[HALF + s] * V_SCALE).astype(BF)

    targets = outs if phase else (outs[0], outs[1], outs[2], outs[3].at[0], outs[3].at[1])
    going = []
    for part in range(4):
        lax.fori_loop(3 * part, 3 * part + 3, lambda s, _: (finish(s), 0)[1], 0)
        rows = pl.ds(3 * part, 3)
        for n, (src, dst) in enumerate(zip(made, targets)):
            going.append(
                pltpu.make_async_copy(src.at[rows], dst.at[rows], sems.at[5 * part + n])
            )
            going[-1].start()
    for copy in going:
        copy.wait()


def piped(ins, shapes, in_sems, outs, staged, out_sems, compute):
    def coming(d):
        rows = pl.ds(3 * d, 3)
        return [
            pltpu.make_async_copy(
                src.at[:, rows] if four else src.at[rows],
                dst.at[:, rows] if four else dst.at[rows],
                in_sems.at[d, n],
            )
            for n, (src, dst, four) in enumerate(zip(ins, shapes[0], shapes[1]))
        ]

    def going(d):
        return pltpu.make_async_copy(staged.at[d], outs[d], out_sems.at[d])

    for d in range(4):
        for copy in coming(d):
            copy.start()
    for d in range(4):
        for copy in coming(d):
            copy.wait()
        compute(d)
        going(d).start()
    for d in range(4):
        going(d).wait()


def sum_kernel(at, *refs):
    ins, outs = refs[:6], refs[6:10]
    bufs, (staged, in_sems, out_sems) = refs[10:16], refs[16:]
    dq, dk, dv, beside, a1, a2 = bufs
    first = at[2] == 0

    def compute(d):
        for m in range(3):
            s = 3 * d + m
            far = a1[s].astype(F32)
            last = jnp.where(first, 0.0, a2[s].astype(F32))
            staged[d, 0, m] = (dq[s].astype(F32) + jnp.where(first, far, 0.0)).astype(BF)
            far = jnp.where(first, 0.0, far)
            staged[d, 1, m] = (dk[s].astype(F32) + beside[0, s].astype(F32) + far).astype(BF)
            staged[d, 2, m] = (dv[s].astype(F32) + beside[1, s].astype(F32) + last).astype(BF)

    piped(ins, (bufs, (0, 0, 0, 1, 0, 0)), in_sems, outs, staged, out_sems, compute)


def join_kernel(arrays, at, *refs):
    outs, (stage, sems) = refs[4 : 4 + arrays], refs[-2:]
    moves = []
    for d in range(4):
        lanes = pl.ds(pl.multiple_of(lax.rem(at[0] + d, 4) * HEAD, HEAD), HEAD)
        moves += [(refs[d].at[n], outs[n].at[:, lanes]) for n in range(arrays)]
    relay(moves, stage, sems)


def call(kernel, outs, ins, scratch=(), limit=56, where=ANY, cost=None, **kw):
    return pl.pallas_call(
        kernel,
        out_shape=outs,
        in_specs=ins,
        out_specs=[where] * len(outs),
        scratch_shapes=scratch,
        compiler_params=pltpu.CompilerParams(vmem_limit_bytes=limit * 2**20),
        cost_estimate=cost,
        **kw,
    )


def table_kernel(at, counts, rows, out):
    y, core, z = at[0], at[2], at[3]
    shape = rows.shape[1:]
    lane = lax.broadcasted_iota(jnp.int32, shape, 1)
    line = lax.broadcasted_iota(jnp.int32, shape, 0)
    spot = lax.broadcasted_iota(jnp.int32, (shape[0], SPOTS), 1)
    ahead = (
        lax.broadcasted_iota(jnp.int32, (128, 128), 0)
        < lax.broadcasted_iota(jnp.int32, (128, 128), 1)
    ).astype(F32)
    above = (
        lax.broadcasted_iota(jnp.int32, (shape[0], shape[0]), 1)
        < lax.broadcasted_iota(jnp.int32, (shape[0], shape[0]), 0)
    ).astype(F32)

    def at_least(a, *bounds):
        return sum((a >= b).astype(jnp.int32) for b in bounds)

    def slot(u):
        third = at_least(u, 3, 6, 9)
        return ((y - third) & 3) * 3 + u - 3 * third

    def place_values(rank, value, columns):
        made = jnp.zeros((shape[0], SPOTS), jnp.int32)
        for j in columns:
            made += jnp.where(rank[:, j : j + 1] == spot, value[:, j : j + 1], 0)
        return jnp.sum(made, 0, keepdims=True)

    for phase in range(2):
        kid = rows[0] if phase else jnp.where(core == 0, rows[1], rows[0])
        kept = jnp.zeros(shape, jnp.int32)
        for k in range(4 * PLANE):
            kept = jnp.where(kid == k, BLK - counts[k], kept)
        plane = at_least(kid, PLANE, 2 * PLANE, 3 * PLANE)
        t = kid - PLANE * plane
        half = at_least(t, HALF)
        listed = (
            at_least(kid, 0) * at_least(lane, 1) * (1 - at_least(lane, KPB)) * (1 - at_least(line, HALF))
        )
        here, same = (plane == z).astype(jnp.int32), (half == core).astype(jnp.int32)
        ks = slot(t - HALF * half)
        if phase:
            valid = listed * here * same
        else:
            above_it = (z < 3).astype(jnp.int32)
            valid = listed * jnp.where(core == 0, here * above_it, 1 - here * same)
            ks = ks + HALF * here * (1 - same)
        cls = jnp.clip(((kept + 31) >> 5) - 5, 0, 3)
        value = slot(line) | (ks << 4) | (kept << 9) | (cls << 18)
        rank, total = jnp.full(shape, -1, jnp.int32), 0
        for c in range(4):
            mine = valid * (cls == c).astype(jnp.int32)
            ones = mine.astype(F32)
            before = nn(ones, ahead) + jnp.sum(nn(above, ones), 1, keepdims=True)
            rank = jnp.where(mine > 0, total + before.astype(jnp.int32), rank)
            total = total + jnp.sum(mine)
        made = place_values(rank, value, range(1, KPB))
        first = spot[:1]
        made = jnp.where(first < total, made, HALF | (DUMMY[phase] << 4) | (3 << 18))
        out[phase : phase + 1] = jnp.where(first == SPOTS - 1, total, made)
        if phase:
            out[2:3] = place_values(jnp.where(line < HALF, slot(line), -1), kept, (0,))


def pairs_cost(pairs):
    return pl.CostEstimate(
        flops=pairs * 10 * BLK * BLK * HEAD, bytes_accessed=12 * 2**20, transcendentals=pairs * BLK * BLK
    )


def body(queries, keys, values, out_grad, key_blocks, target_counts):
    ctx, tp = lax.axis_index("ctx"), lax.axis_index("tp")
    z, x, y, core = ctx // 8, (ctx // 4) % 2, ctx % 4, tp % 2
    at = jnp.stack([y, x, core, z]).astype(jnp.int32)
    rows = queries.shape[0]
    shape = jax.ShapeDtypeStruct
    dma = lambda *n: pltpu.SemaphoreType.DMA(n)
    own = lax.dynamic_slice(key_blocks, (PLANE * z + HALF * core, 0), (HALF, KPB))
    after = lax.dynamic_slice(key_blocks, (jnp.minimum(PLANE * (z + 1), 84), 0), (HALF, KPB))
    lists = jnp.pad(jnp.stack([own, after]), ((0, 0), (0, 4), (0, 128 - KPB)), constant_values=-1)
    tab = call(
        table_kernel,
        [shape((3, SPOTS), jnp.int32)],
        [SMEM, SMEM, VMEM],
        where=VMEM,
        name="table",
    )(at, target_counts, lists)[0]
    half = shape((HALF, BLK, HEAD), BF)

    def split(first_round, *behind):
        return call(
            functools.partial(split_kernel, first_round),
            [shape((2, rows, HEAD), BF)] * 4,
            [SMEM] + [ANY] * (4 + len(behind)),
            [pltpu.VMEM((8, rows, HEAD), BF), dma(2, 8)],
            limit=56,
            name="split",
        )(at, queries, out_grad, keys, values, *behind)

    def send(pieces, pairs):
        return [lax.ppermute(p, AXES, pairs(d)) for d, p in enumerate(pieces)]

    two = shape((2, HALF, BLK, HEAD), BF)


    def blocks(pieces):
        return [p.reshape(2, 3, BLK, HEAD) for p in pieces]

    sent1 = split(True)
    sent2 = split(False, sent1[0], tab)
    r1 = blocks(send(sent1, to_heads))
    r2 = blocks(send(sent2, to_heads))
    first = call(
        gather_kernel,
        [two],
        [ANY] * 5,
        [pltpu.VMEM((4, 2, 3, BLK, HEAD), BF), dma(2, 4)],
        name="gather",
    )(*r1, sent2[0])[0]
    across = lax.ppermute(first, AXES, ALONG_Z)
    near = call(
        gather_keys_kernel,
        [shape((2, n, BLK, HEAD), BF) for n in (MOST, HALF - MOST)],
        [SMEM] + [ANY] * 8,
        [pltpu.VMEM((HALF, 2, BLK, HEAD), BF), dma(2, HALF)],
        name="gather_keys",
    )(at, *r1, *r2)
    near = [lax.ppermute(n, AXES, OTHER_CORE) for n in near]

    def scratch(k):
        return [
            pltpu.VMEM((HALF + 1, BLK, HEAD), BF),
            pltpu.VMEM((HALF + 1, BLK, HEAD), BF),
            pltpu.VMEM((k + 1, BLK, HEAD), BF),
            pltpu.VMEM((k + 1, BLK, HEAD), BF),
            pltpu.VMEM((HALF + 1, HEAD, BLK), F32),
            pltpu.VMEM((k + 1, BLK, HEAD), F32),
            pltpu.VMEM((k + 1, BLK, HEAD), F32),
        ]

    parts = [pltpu.VMEM((HALF, BLK, HEAD), BF)] * 5
    p1, p2, s1, beside = call(
        functools.partial(pairs_kernel, 0),
        [half, half, half, two],
        [SMEM] * 2 + [ANY] * 11,
        parts + scratch(PLANE) + [dma(44)],
        cost=pairs_cost(139),
        limit=56,
        name="far",
    )(at, tab, *r1, *r2, across, *near)
    s2 = p2
    p1 = lax.ppermute(p1, AXES, BACK_Z)
    p2 = lax.ppermute(p2, AXES, BACK_Z_SECOND)
    beside = lax.ppermute(beside, AXES, OTHER_CORE)
    dq, dk, dv = call(
        functools.partial(pairs_kernel, 1),
        [half, half, half],
        [SMEM] * 2 + [ANY] * 10,
        parts + scratch(HALF) + [dma(44)],
        cost=pairs_cost(60),
        limit=56,
        name="own",
    )(at, tab, *r1, *r2, s1, s2)
    v3, v4 = pltpu.VMEM((HALF, BLK, HEAD), BF), pltpu.VMEM((2, HALF, BLK, HEAD), BF)
    sums = call(
        sum_kernel,
        [shape((3, 3, BLK, HEAD), BF)] * 4,
        [SMEM] + [ANY] * 6,
        [v3, v3, v3, v4, v3, v3, pltpu.VMEM((4, 3, 3, BLK, HEAD), BF), dma(4, 6), dma(4)],
        limit=56,
        name="sums",
    )(at, dq, dk, dv, beside, p1, p2)
    back = send([p.reshape(3, rows, HEAD) for p in sums], from_heads)
    out = shape(queries.shape, BF)
    return tuple(
        call(
            functools.partial(join_kernel, 3),
            [out] * 3,
            [SMEM] + [ANY] * 4,
            [pltpu.VMEM((12, rows, HEAD), BF), dma(2, 12)],
            name="join",
        )(at, *back)
    )


def solution(mesh):
    in_specs = (P("ctx", "tp"),) * 4 + (P(), P())
    return jax.shard_map(
        body, mesh=mesh, in_specs=in_specs, out_specs=(P("ctx", "tp"),) * 3, check_vma=False
    )
```

```python
import functools
import math

import jax
import jax.numpy as jnp
from jax import lax
from jax.experimental import pallas as pl
from jax.experimental.pallas import tpu as pltpu
from jax.sharding import PartitionSpec as P

F32, BF = jnp.float32, jnp.bfloat16
HEAD, BLK, KPB = 128, 256, 16
PLANE, HALF = 24, 12
AXES = ("ctx", "tp")
U_SCALE = 0.5 / math.sqrt(HEAD)
V_SCALE = 1.0 / math.sqrt(KPB * BLK)
QK_SCALE = 0.5 * V_SCALE / math.sqrt(HEAD)
GROUP = (8, 6)
CLASSES = (160, 192, 224, 256)
SPOTS = 256
MOST = 10
DUMMY = (24, 12)
VMEM = pl.BlockSpec(memory_space=pltpu.VMEM)
SMEM = pl.BlockSpec(memory_space=pltpu.SMEM)
ANY = pl.BlockSpec(memory_space=pl.ANY)


def place(z, x, y, hi, core):
    return (z * 8 + x * 4 + y % 4) * 4 + hi * 2 + core


DEVICES = [
    (z, x, y, hi, core)
    for z in range(4)
    for x in range(2)
    for y in range(4)
    for hi in range(2)
    for core in range(2)
]


def to_heads(d):
    return [(place(z, x, y, hi, c), place(z, c, y + d, hi, x)) for z, x, y, hi, c in DEVICES]


def from_heads(d):
    return [(j, i) for i, j in to_heads(d)]


OTHER_CORE = [(place(z, x, y, hi, c), place(z, x, y, hi, 1 - c)) for z, x, y, hi, c in DEVICES]
ALONG_Z = [
    (place(z, x, y, hi, c), place(z + 2 * c - 1, x, y, hi, c))
    for z, x, y, hi, c in DEVICES
    if 0 <= z + 2 * c - 1 < 4
]
BACK_Z = [(j, i) for i, j in ALONG_Z]


def nt(a, b):
    return lax.dot_general(a, b, (((1,), (1,)), ((), ())), preferred_element_type=F32)


def nn(a, b):
    return lax.dot_general(a, b, (((1,), (0,)), ((), ())), preferred_element_type=F32)


def tn(a, b):
    return lax.dot_general(a, b, (((0,), (0,)), ((), ())), preferred_element_type=F32)


def relay(moves, stage, sems):
    ins = [
        pltpu.make_async_copy(src, stage.at[n], sems.at[0, n]) for n, (src, _) in enumerate(moves)
    ]
    outs = [
        pltpu.make_async_copy(stage.at[n], dst, sems.at[1, n]) for n, (_, dst) in enumerate(moves)
    ]
    for copy in ins:
        copy.start()
    for n, copy in enumerate(ins):
        copy.wait()
        outs[n].start()
    for copy in outs:
        copy.wait()


def split_kernel(first_round, at, q, g, k, v, *refs):
    outs, (stage, sems) = refs[-6:-2], refs[-2:]
    y, x = at[0], at[1]
    for side, pair in ((0, (q, g)), (1, (k, v))):

        @pl.when(x == (side if first_round else 1 - side))
        def _(pair=pair):
            moves = []
            for d in range(4):
                lanes = pl.ds(pl.multiple_of(lax.rem(y + d, 4) * HEAD, HEAD), HEAD)
                moves += [(pair[n].at[:, lanes], outs[d].at[n]) for n in range(2)]
            relay(moves, stage, sems)


def gather_kernel(*refs):
    ins, (out, stage, sems) = refs[:4], refs[-3:]
    relay([(ins[d], out.at[:, pl.ds(3 * d, 3)]) for d in range(4)], stage, sems)


def gather_keys_kernel(at, *refs):
    ins, (most, rest, stage, sems) = refs[:8], refs[8:]
    for own, pieces in ((0, ins[4:]), (1, ins[:4])):

        @pl.when(at[2] == own)
        def _(pieces=pieces):
            moves = []
            for d in range(4):
                for m in range(3):
                    b = 3 * d + m
                    to = most.at[:, b] if b < MOST else rest.at[:, b - MOST]
                    moves.append((pieces[d].at[:, m], to))
            relay(moves, stage, sems)


def pair_grads(scores, weight_grad, allowed):
    u = scores * U_SCALE
    t = jnp.tanh(u)
    p = 1.0 + t
    if allowed is not None:
        p = jnp.where(allowed, p, 0.0)
    w = u * p
    slope = p + w * (1.0 - t)
    return w.astype(BF), (weight_grad * slope).astype(BF)


def pairs_kernel(phase, at, tab, *refs):
    r1, r2 = refs[0:4], refs[4:8]
    extra = refs[8:10] if phase else refs[8:11]
    refs = refs[10:] if phase else refs[11:]
    if phase:
        outs, refs = refs[:3], refs[3:]
        (*made, s1, s2), refs = refs[:5], refs[5:]
    else:
        outs, refs = refs[:3], refs[3:]
        made, refs = refs[:5], refs[5:]
    qs, gs, ks, vs, dqa, dka, dva, sems = refs
    core, size = at[2], GROUP[phase]
    groups = (tab[phase, SPOTS - 1] + size - 1) // size

    def copies(own):
        qg, kv = ((r1, r2), (r2, r1))[own]
        out = []
        for d in range(4):
            rows = pl.ds(3 * d, 3)
            if phase == 1 or own == 1:
                out += [(qg[d].at[0], qs.at[rows]), (qg[d].at[1], gs.at[rows])]
            if phase == 1 or own == 0:
                out += [(kv[d].at[0], ks.at[rows]), (kv[d].at[1], vs.at[rows])]
        if phase == 0:
            across, most, rest = extra
            to = (ks, vs) if own else (qs, gs)
            for n in range(2):
                out.append((across.at[n], to[n].at[pl.ds(0, HALF)]))
                out.append((most.at[n], (ks, vs)[n].at[pl.ds(HALF, MOST)]))
                out.append((rest.at[n], (ks, vs)[n].at[pl.ds(HALF + MOST, HALF - MOST)]))
        return [pltpu.make_async_copy(a, b, sems.at[i]) for i, (a, b) in enumerate(out)]

    def late():
        return [
            pltpu.make_async_copy(extra[0], s1, sems.at[42]),
            pltpu.make_async_copy(extra[1].at[1], s2, sems.at[43]),
        ]

    for own in range(2):

        @pl.when(core == own)
        def _(own=own):
            for copy in copies(own):
                copy.start()

    if phase:
        for copy in late():
            copy.start()
    dqa[...] = jnp.zeros_like(dqa)
    dka[...] = jnp.zeros_like(dka)
    dva[...] = jnp.zeros_like(dva)
    zero = jnp.zeros((BLK, HEAD), BF)
    dummy = DUMMY[phase]
    qs[HALF], gs[HALF], ks[dummy], vs[dummy] = zero, zero, zero, zero

    for own in range(2):

        @pl.when(core == own)
        def _(own=own):
            for copy in copies(own):
                copy.wait()

    def work(items, rows):
        def scores(item):
            q, k, mask = item
            key, value, query, grad = ks[k, :rows], vs[k, :rows], qs[q], gs[q]
            return q, k, mask, key, query, grad, nt(key, query), nt(value, grad)

        def grads(q, k, mask, key, query, grad, score, weight_grad):
            made = [
                pair_grads(score[lo:hi], weight_grad[lo:hi], mask(lo, hi))
                for lo, hi in ((0, 128), (128, rows))
            ]
            w, sg = (jnp.concatenate(parts) for parts in zip(*made))
            dva[k, :rows] += nn(w, grad)
            dka[k, :rows] += nn(sg, query)
            dqa[q] += tn(key, sg)

        ahead = scores(items[0])
        for item in (*items[1:], None):
            now, ahead = ahead, None if item is None else scores(item)
            grads(*now)

    def own_group(g, _):
        def mask_of(slot):
            def mask(lo, hi):
                row = lo + lax.broadcasted_iota(jnp.int32, (hi - lo, BLK), 0)
                col = lax.broadcasted_iota(jnp.int32, (hi - lo, BLK), 1)
                return (row == col) | ((row < col) & (row < tab[2, slot]))

            return mask

        slots = [g * 6 + i for i in range(6)]
        work([(slot, slot, mask_of(slot)) for slot in slots], BLK)
        return 0

    if phase:
        lax.fori_loop(0, 2, own_group, 0)

    def mask_from(kept):
        def mask(lo, hi):
            if lo == 0:
                return None
            return lo + lax.broadcasted_iota(jnp.int32, (hi - lo, BLK), 0) < kept

        return mask

    def group(g, _):
        for c, rows in enumerate(CLASSES):

            @pl.when((tab[phase, g * size + size - 1] >> 18) == c)
            def _(rows=rows):
                items = []
                for i in range(size):
                    e = tab[phase, g * size + i]
                    items.append((e & 15, (e >> 4) & 31, mask_from((e >> 9) & 511)))
                work(items, rows)

        return 0

    lax.fori_loop(0, groups, group, 0)

    if phase:
        for copy in late():
            copy.wait()

    def finish(s):
        dq, dk, dv = dqa[s].T * QK_SCALE, dka[s] * QK_SCALE, dva[s] * V_SCALE
        if phase:
            before, last = s1[s].astype(F32), s2[s].astype(F32)
            made[0][s] = (dq + jnp.where(core == 1, before, 0.0)).astype(BF)
            made[1][s] = (dk + jnp.where(core == 0, before, 0.0)).astype(BF)
            made[2][s] = (dv + jnp.where(core == 0, last, 0.0)).astype(BF)
        else:
            made[0][s] = jnp.where(core == 0, dq, dk).astype(BF)
            made[1][s] = dv.astype(BF)
            made[2][s] = jnp.where(core == 0, dk, dq).astype(BF)
            made[3][s] = (dka[HALF + s] * QK_SCALE).astype(BF)
            made[4][s] = (dva[HALF + s] * V_SCALE).astype(BF)

    targets = outs
    if phase == 0:
        targets = (outs[0].at[0], outs[0].at[1], outs[1], outs[2].at[0], outs[2].at[1])
    going = []
    for part in range(4):
        lax.fori_loop(3 * part, 3 * part + 3, lambda s, _: (finish(s), 0)[1], 0)
        rows = pl.ds(3 * part, 3)
        for n, (src, dst) in enumerate(zip(made, targets)):
            going.append(
                pltpu.make_async_copy(src.at[rows], dst.at[rows], sems.at[5 * part + n])
            )
            going[-1].start()
    for copy in going:
        copy.wait()


def sum_kernel(at, *refs):
    (beside, back), ins, outs = refs[:2], refs[2:5], refs[5:9]
    bufs, (staged, in_sems, out_sems) = refs[9:12], refs[12:]
    dq, dk, dv = bufs
    first = at[2] == 0

    def coming(d):
        rows = pl.ds(3 * d, 3)
        return [
            pltpu.make_async_copy(src.at[rows], dst.at[rows], in_sems.at[d, n])
            for n, (src, dst) in enumerate(zip(ins, bufs))
        ]

    def going(d):
        return pltpu.make_async_copy(staged.at[d], outs[d], out_sems.at[d])

    for d in range(4):
        for copy in coming(d):
            copy.start()
    for d in range(4):
        for copy in coming(d):
            copy.wait()
        for m in range(3):
            s = 3 * d + m
            far = back[0, s].astype(F32)
            last = jnp.where(first, 0.0, back[1, s].astype(F32))
            staged[d, 0, m] = (dq[s].astype(F32) + jnp.where(first, far, 0.0)).astype(BF)
            far = jnp.where(first, 0.0, far)
            staged[d, 1, m] = (dk[s].astype(F32) + beside[0, s].astype(F32) + far).astype(BF)
            staged[d, 2, m] = (dv[s].astype(F32) + beside[1, s].astype(F32) + last).astype(BF)
        going(d).start()
    for d in range(4):
        going(d).wait()


def join_kernel(arrays, at, *refs):
    outs, sems = refs[4 : 4 + arrays], refs[-1]
    copies = []
    for d in range(4):
        lanes = pl.ds(pl.multiple_of(lax.rem(at[0] + d, 4) * HEAD, HEAD), HEAD)
        for n in range(arrays):
            copies.append(
                pltpu.make_async_copy(refs[d].at[n], outs[n].at[:, lanes], sems.at[arrays * d + n])
            )
    for copy in copies:
        copy.start()
    for copy in copies:
        copy.wait()


def call(kernel, outs, ins, scratch=(), limit=56, where=ANY, cost=None, **kw):
    return pl.pallas_call(
        kernel,
        out_shape=outs,
        in_specs=ins,
        out_specs=[where] * len(outs),
        scratch_shapes=scratch,
        compiler_params=pltpu.CompilerParams(vmem_limit_bytes=limit * 2**20),
        cost_estimate=cost,
        **kw,
    )


def table_kernel(at, counts, rows, out):
    y, core, z = at[0], at[2], at[3]
    shape = rows.shape[1:]
    lane = lax.broadcasted_iota(jnp.int32, shape, 1)
    line = lax.broadcasted_iota(jnp.int32, shape, 0)
    spot = lax.broadcasted_iota(jnp.int32, (shape[0], SPOTS), 1)
    ahead = (
        lax.broadcasted_iota(jnp.int32, (128, 128), 0)
        < lax.broadcasted_iota(jnp.int32, (128, 128), 1)
    ).astype(F32)
    above = (
        lax.broadcasted_iota(jnp.int32, (shape[0], shape[0]), 1)
        < lax.broadcasted_iota(jnp.int32, (shape[0], shape[0]), 0)
    ).astype(F32)

    def at_least(a, *bounds):
        return sum((a >= b).astype(jnp.int32) for b in bounds)

    def slot(u):
        third = at_least(u, 3, 6, 9)
        return ((y - third) & 3) * 3 + u - 3 * third

    def place_values(rank, value, columns):
        made = jnp.zeros((shape[0], SPOTS), jnp.int32)
        for j in columns:
            made += jnp.where(rank[:, j : j + 1] == spot, value[:, j : j + 1], 0)
        return jnp.sum(made, 0, keepdims=True)

    for phase in range(2):
        kid = rows[0] if phase else jnp.where(core == 0, rows[1], rows[0])
        kept = jnp.zeros(shape, jnp.int32)
        for k in range(4 * PLANE):
            kept = jnp.where(kid == k, BLK - counts[k], kept)
        plane = at_least(kid, PLANE, 2 * PLANE, 3 * PLANE)
        t = kid - PLANE * plane
        half = at_least(t, HALF)
        listed = (
            at_least(kid, 0) * at_least(lane, 1) * (1 - at_least(lane, KPB)) * (1 - at_least(line, HALF))
        )
        here, same = (plane == z).astype(jnp.int32), (half == core).astype(jnp.int32)
        ks = slot(t - HALF * half)
        if phase:
            valid = listed * here * same
        else:
            above_it = (z < 3).astype(jnp.int32)
            valid = listed * jnp.where(core == 0, here * above_it, 1 - here * same)
            ks = ks + HALF * here * (1 - same)
        cls = jnp.clip(((kept + 31) >> 5) - 5, 0, 3)
        value = slot(line) | (ks << 4) | (kept << 9) | (cls << 18)
        rank, total = jnp.full(shape, -1, jnp.int32), 0
        for c in range(4):
            mine = valid * (cls == c).astype(jnp.int32)
            ones = mine.astype(F32)
            before = nn(ones, ahead) + jnp.sum(nn(above, ones), 1, keepdims=True)
            rank = jnp.where(mine > 0, total + before.astype(jnp.int32), rank)
            total = total + jnp.sum(mine)
        made = place_values(rank, value, range(1, KPB))
        first = spot[:1]
        made = jnp.where(first < total, made, HALF | (DUMMY[phase] << 4) | (3 << 18))
        out[phase : phase + 1] = jnp.where(first == SPOTS - 1, total, made)
        if phase:
            out[2:3] = place_values(jnp.where(line < HALF, slot(line), -1), kept, (0,))


def pairs_cost(pairs):
    return pl.CostEstimate(
        flops=pairs * 10 * BLK * BLK * HEAD, bytes_accessed=12 * 2**20, transcendentals=pairs * BLK * BLK
    )


def body(queries, keys, values, out_grad, key_blocks, target_counts):
    ctx, tp = lax.axis_index("ctx"), lax.axis_index("tp")
    z, x, y, core = ctx // 8, (ctx // 4) % 2, ctx % 4, tp % 2
    at = jnp.stack([y, x, core, z]).astype(jnp.int32)
    rows = queries.shape[0]
    shape = jax.ShapeDtypeStruct
    dma = lambda *n: pltpu.SemaphoreType.DMA(n)
    own = lax.dynamic_slice(key_blocks, (PLANE * z + HALF * core, 0), (HALF, KPB))
    after = lax.dynamic_slice(key_blocks, (jnp.minimum(PLANE * (z + 1), 84), 0), (HALF, KPB))
    lists = jnp.pad(jnp.stack([own, after]), ((0, 0), (0, 4), (0, 128 - KPB)), constant_values=-1)
    tab = call(
        table_kernel,
        [shape((3, SPOTS), jnp.int32)],
        [SMEM, SMEM, VMEM],
        where=VMEM,
        name="table",
    )(at, target_counts, lists)[0]
    half = shape((HALF, BLK, HEAD), BF)

    def split(first_round, *behind):
        return call(
            functools.partial(split_kernel, first_round),
            [shape((2, rows, HEAD), BF)] * 4,
            [SMEM] + [ANY] * (4 + len(behind)),
            [pltpu.VMEM((8, rows, HEAD), BF), dma(2, 8)],
            limit=56,
            name="split",
        )(at, queries, out_grad, keys, values, *behind)

    def send(pieces, pairs):
        return [lax.ppermute(p, AXES, pairs(d)) for d, p in enumerate(pieces)]

    two = shape((2, HALF, BLK, HEAD), BF)


    def blocks(pieces):
        return [p.reshape(2, 3, BLK, HEAD) for p in pieces]

    sent1 = split(True)
    sent2 = split(False, sent1[0], tab)
    r1 = blocks(send(sent1, to_heads))
    r2 = blocks(send(sent2, to_heads))
    first = call(
        gather_kernel,
        [two],
        [ANY] * 5,
        [pltpu.VMEM((4, 2, 3, BLK, HEAD), BF), dma(2, 4)],
        name="gather",
    )(*r1, sent2[0])[0]
    across = lax.ppermute(first, AXES, ALONG_Z)
    near = call(
        gather_keys_kernel,
        [shape((2, n, BLK, HEAD), BF) for n in (MOST, HALF - MOST)],
        [SMEM] + [ANY] * 8,
        [pltpu.VMEM((HALF, 2, BLK, HEAD), BF), dma(2, HALF)],
        name="gather_keys",
    )(at, *r1, *r2)
    near = [lax.ppermute(n, AXES, OTHER_CORE) for n in near]

    def scratch(k):
        return [
            pltpu.VMEM((HALF + 1, BLK, HEAD), BF),
            pltpu.VMEM((HALF + 1, BLK, HEAD), BF),
            pltpu.VMEM((k + 1, BLK, HEAD), BF),
            pltpu.VMEM((k + 1, BLK, HEAD), BF),
            pltpu.VMEM((HALF + 1, HEAD, BLK), F32),
            pltpu.VMEM((k + 1, BLK, HEAD), F32),
            pltpu.VMEM((k + 1, BLK, HEAD), F32),
        ]

    parts = [pltpu.VMEM((HALF, BLK, HEAD), BF)] * 5
    far, s1, beside = call(
        functools.partial(pairs_kernel, 0),
        [two, half, two],
        [SMEM] * 2 + [ANY] * 11,
        parts + scratch(PLANE) + [dma(44)],
        cost=pairs_cost(139),
        limit=56,
        name="far",
    )(at, tab, *r1, *r2, across, *near)
    back = lax.ppermute(far, AXES, BACK_Z)
    beside = lax.ppermute(beside, AXES, OTHER_CORE)
    dq, dk, dv = call(
        functools.partial(pairs_kernel, 1),
        [half, half, half],
        [SMEM] * 2 + [ANY] * 10,
        parts + scratch(HALF) + [dma(44)],
        cost=pairs_cost(60),
        limit=56,
        name="own",
    )(at, tab, *r1, *r2, s1, far)
    v3 = pltpu.VMEM((HALF, BLK, HEAD), BF)
    sums = call(
        sum_kernel,
        [shape((3, 3, BLK, HEAD), BF)] * 4,
        [SMEM] + [VMEM] * 2 + [ANY] * 3,
        [v3, v3, v3, pltpu.VMEM((4, 3, 3, BLK, HEAD), BF), dma(4, 3), dma(4)],
        limit=56,
        name="sums",
    )(at, beside, back, dq, dk, dv)
    back = send([p.reshape(3, rows, HEAD) for p in sums], from_heads)
    out = shape(queries.shape, BF)
    return tuple(
        call(
            functools.partial(join_kernel, 3),
            [out] * 3,
            [SMEM] + [VMEM] * 4,
            [dma(12)],
            limit=40,
            name="join",
        )(at, *back)
    )


def solution(mesh):
    in_specs = (P("ctx", "tp"),) * 4 + (P(), P())
    return jax.shard_map(
        body, mesh=mesh, in_specs=in_specs, out_specs=(P("ctx", "tp"),) * 3, check_vma=False
    )
```

```python
import functools
import math

import jax
import jax.numpy as jnp
from jax import lax
from jax.experimental import pallas as pl
from jax.experimental.pallas import tpu as pltpu
from jax.sharding import PartitionSpec as P

F32, BF = jnp.float32, jnp.bfloat16
HEAD, BLK, KPB = 128, 256, 16
PLANE, HALF = 24, 12
AXES = ("ctx", "tp")
U_SCALE = 0.5 / math.sqrt(HEAD)
V_SCALE = 1.0 / math.sqrt(KPB * BLK)
QK_SCALE = 0.5 * V_SCALE / math.sqrt(HEAD)
GROUP = (8, 6)
CLASSES = (160, 192, 224, 256)
SPOTS = 256
MOST = 10
DUMMY = (24, 12)
VMEM = pl.BlockSpec(memory_space=pltpu.VMEM)
SMEM = pl.BlockSpec(memory_space=pltpu.SMEM)
ANY = pl.BlockSpec(memory_space=pl.ANY)


def place(z, x, y, hi, core):
    return (z * 8 + x * 4 + y % 4) * 4 + hi * 2 + core


DEVICES = [
    (z, x, y, hi, core)
    for z in range(4)
    for x in range(2)
    for y in range(4)
    for hi in range(2)
    for core in range(2)
]


def to_heads(d):
    return [(place(z, x, y, hi, c), place(z, c, y + d, hi, x)) for z, x, y, hi, c in DEVICES]


def from_heads(d):
    return [(j, i) for i, j in to_heads(d)]


OTHER_CORE = [(place(z, x, y, hi, c), place(z, x, y, hi, 1 - c)) for z, x, y, hi, c in DEVICES]
ALONG_Z = [
    (place(z, x, y, hi, c), place(z + 2 * c - 1, x, y, hi, c))
    for z, x, y, hi, c in DEVICES
    if 0 <= z + 2 * c - 1 < 4
]
BACK_Z = [(j, i) for i, j in ALONG_Z]


def nt(a, b):
    return lax.dot_general(a, b, (((1,), (1,)), ((), ())), preferred_element_type=F32)


def nn(a, b):
    return lax.dot_general(a, b, (((1,), (0,)), ((), ())), preferred_element_type=F32)


def tn(a, b):
    return lax.dot_general(a, b, (((0,), (0,)), ((), ())), preferred_element_type=F32)


def relay(moves, stage, sems):
    ins = [
        pltpu.make_async_copy(src, stage.at[n], sems.at[0, n]) for n, (src, _) in enumerate(moves)
    ]
    outs = [
        pltpu.make_async_copy(stage.at[n], dst, sems.at[1, n]) for n, (_, dst) in enumerate(moves)
    ]
    for copy in ins:
        copy.start()
    for n, copy in enumerate(ins):
        copy.wait()
        outs[n].start()
    for copy in outs:
        copy.wait()


def split_kernel(first_round, at, q, g, k, v, *refs):
    outs, (stage, sems) = refs[-6:-2], refs[-2:]
    y, x = at[0], at[1]
    for side, pair in ((0, (q, g)), (1, (k, v))):

        @pl.when(x == (side if first_round else 1 - side))
        def _(pair=pair):
            moves = []
            for d in range(4):
                lanes = pl.ds(pl.multiple_of(lax.rem(y + d, 4) * HEAD, HEAD), HEAD)
                moves += [(pair[n].at[:, lanes], outs[d].at[n]) for n in range(2)]
            relay(moves, stage, sems)


def gather_kernel(*refs):
    ins, (out, stage, sems) = refs[:4], refs[-3:]
    relay([(ins[d], out.at[:, pl.ds(3 * d, 3)]) for d in range(4)], stage, sems)


def gather_keys_kernel(at, *refs):
    ins, (most, rest, stage, sems) = refs[:8], refs[8:]
    for own, pieces in ((0, ins[4:]), (1, ins[:4])):

        @pl.when(at[2] == own)
        def _(pieces=pieces):
            moves = []
            for d in range(4):
                for m in range(3):
                    b = 3 * d + m
                    to = most.at[:, b] if b < MOST else rest.at[:, b - MOST]
                    moves.append((pieces[d].at[:, m], to))
            relay(moves, stage, sems)


def pair_grads(scores, weight_grad, allowed):
    u = scores * U_SCALE
    t = jnp.tanh(u)
    p = 1.0 + t
    if allowed is not None:
        p = jnp.where(allowed, p, 0.0)
    w = u * p
    slope = p + w * (1.0 - t)
    return w.astype(BF), (weight_grad * slope).astype(BF)


def pairs_kernel(phase, at, tab, *refs):
    r1, r2 = refs[0:4], refs[4:8]
    extra = refs[8:10] if phase else refs[8:11]
    refs = refs[10:] if phase else refs[11:]
    if phase:
        outs, refs = refs[:3], refs[3:]
        (*made, s1, s2), refs = refs[:5], refs[5:]
    else:
        outs, refs = refs[:3], refs[3:]
        made, refs = refs[:5], refs[5:]
    qs, gs, ks, vs, dqa, dka, dva, sems = refs
    core, size = at[2], GROUP[phase]
    groups = (tab[phase, SPOTS - 1] + size - 1) // size

    def copies(own):
        qg, kv = ((r1, r2), (r2, r1))[own]
        out = []
        for d in range(4):
            rows = pl.ds(3 * d, 3)
            if phase == 1 or own == 1:
                out += [(qg[d].at[0], qs.at[rows]), (qg[d].at[1], gs.at[rows])]
            if phase == 1 or own == 0:
                out += [(kv[d].at[0], ks.at[rows]), (kv[d].at[1], vs.at[rows])]
        if phase == 0:
            across, most, rest = extra
            to = (ks, vs) if own else (qs, gs)
            for n in range(2):
                out.append((across.at[n], to[n].at[pl.ds(0, HALF)]))
                out.append((most.at[n], (ks, vs)[n].at[pl.ds(HALF, MOST)]))
                out.append((rest.at[n], (ks, vs)[n].at[pl.ds(HALF + MOST, HALF - MOST)]))
        return [pltpu.make_async_copy(a, b, sems.at[i]) for i, (a, b) in enumerate(out)]

    def late():
        return [
            pltpu.make_async_copy(extra[0], s1, sems.at[42]),
            pltpu.make_async_copy(extra[1].at[1], s2, sems.at[43]),
        ]

    for own in range(2):

        @pl.when(core == own)
        def _(own=own):
            for copy in copies(own):
                copy.start()

    if phase:
        for copy in late():
            copy.start()
    dqa[...] = jnp.zeros_like(dqa)
    dka[...] = jnp.zeros_like(dka)
    dva[...] = jnp.zeros_like(dva)
    zero = jnp.zeros((BLK, HEAD), BF)
    dummy = DUMMY[phase]
    qs[HALF], gs[HALF], ks[dummy], vs[dummy] = zero, zero, zero, zero

    for own in range(2):

        @pl.when(core == own)
        def _(own=own):
            for copy in copies(own):
                copy.wait()

    def work(items, rows):
        def scores(item):
            q, k, mask = item
            key, value, query, grad = ks[k, :rows], vs[k, :rows], qs[q], gs[q]
            return q, k, mask, key, query, grad, nt(key, query), nt(value, grad)

        def grads(q, k, mask, key, query, grad, score, weight_grad):
            made = [
                pair_grads(score[lo:hi], weight_grad[lo:hi], mask(lo, hi))
                for lo, hi in ((0, 128), (128, rows))
            ]
            w, sg = (jnp.concatenate(parts) for parts in zip(*made))
            dva[k, :rows] += nn(w, grad)
            dka[k, :rows] += nn(sg, query)
            dqa[q] += tn(key, sg)

        ahead = scores(items[0])
        for item in (*items[1:], None):
            now, ahead = ahead, None if item is None else scores(item)
            grads(*now)

    def own_group(g, _):
        def mask_of(slot):
            def mask(lo, hi):
                row = lo + lax.broadcasted_iota(jnp.int32, (hi - lo, BLK), 0)
                col = lax.broadcasted_iota(jnp.int32, (hi - lo, BLK), 1)
                return (row == col) | ((row < col) & (row < tab[2, slot]))

            return mask

        slots = [g * 6 + i for i in range(6)]
        work([(slot, slot, mask_of(slot)) for slot in slots], BLK)
        return 0

    if phase:
        lax.fori_loop(0, 2, own_group, 0)

    def mask_from(kept):
        def mask(lo, hi):
            if lo == 0:
                return None
            return lo + lax.broadcasted_iota(jnp.int32, (hi - lo, BLK), 0) < kept

        return mask

    def group(g, _):
        for c, rows in enumerate(CLASSES):

            @pl.when((tab[phase, g * size + size - 1] >> 18) == c)
            def _(rows=rows):
                items = []
                for i in range(size):
                    e = tab[phase, g * size + i]
                    items.append((e & 15, (e >> 4) & 31, mask_from((e >> 9) & 511)))
                work(items, rows)

        return 0

    lax.fori_loop(0, groups, group, 0)

    if phase:
        for copy in late():
            copy.wait()

    def finish(s):
        dq, dk, dv = dqa[s].T * QK_SCALE, dka[s] * QK_SCALE, dva[s] * V_SCALE
        if phase:
            before, last = s1[s].astype(F32), s2[s].astype(F32)
            made[0][s] = (dq + jnp.where(core == 1, before, 0.0)).astype(BF)
            made[1][s] = (dk + jnp.where(core == 0, before, 0.0)).astype(BF)
            made[2][s] = (dv + jnp.where(core == 0, last, 0.0)).astype(BF)
        else:
            made[0][s] = jnp.where(core == 0, dq, dk).astype(BF)
            made[1][s] = dv.astype(BF)
            made[2][s] = jnp.where(core == 0, dk, dq).astype(BF)
            made[3][s] = (dka[HALF + s] * QK_SCALE).astype(BF)
            made[4][s] = (dva[HALF + s] * V_SCALE).astype(BF)

    targets = outs
    if phase == 0:
        targets = (outs[0].at[0], outs[0].at[1], outs[1], outs[2].at[0], outs[2].at[1])
    going = []
    for part in range(4):
        lax.fori_loop(3 * part, 3 * part + 3, lambda s, _: (finish(s), 0)[1], 0)
        rows = pl.ds(3 * part, 3)
        for n, (src, dst) in enumerate(zip(made, targets)):
            going.append(
                pltpu.make_async_copy(src.at[rows], dst.at[rows], sems.at[5 * part + n])
            )
            going[-1].start()
    for copy in going:
        copy.wait()


def sum_kernel(at, *refs):
    (beside, back), ins, outs = refs[:2], refs[2:5], refs[5:9]
    bufs, (staged, in_sems, out_sems) = refs[9:12], refs[12:]
    dq, dk, dv = bufs
    first = at[2] == 0

    def coming(d):
        rows = pl.ds(3 * d, 3)
        return [
            pltpu.make_async_copy(src.at[rows], dst.at[rows], in_sems.at[d, n])
            for n, (src, dst) in enumerate(zip(ins, bufs))
        ]

    def going(d):
        return pltpu.make_async_copy(staged.at[d], outs[d], out_sems.at[d])

    for d in range(4):
        for copy in coming(d):
            copy.start()
    for d in range(4):
        for copy in coming(d):
            copy.wait()
        for m in range(3):
            s = 3 * d + m
            far = back[0, s].astype(F32)
            last = jnp.where(first, 0.0, back[1, s].astype(F32))
            staged[d, 0, m] = (dq[s].astype(F32) + jnp.where(first, far, 0.0)).astype(BF)
            far = jnp.where(first, 0.0, far)
            staged[d, 1, m] = (dk[s].astype(F32) + beside[0, s].astype(F32) + far).astype(BF)
            staged[d, 2, m] = (dv[s].astype(F32) + beside[1, s].astype(F32) + last).astype(BF)
        going(d).start()
    for d in range(4):
        going(d).wait()


def join_kernel(arrays, at, *refs):
    outs, sems = refs[4 : 4 + arrays], refs[-1]
    copies = []
    for d in range(4):
        lanes = pl.ds(pl.multiple_of(lax.rem(at[0] + d, 4) * HEAD, HEAD), HEAD)
        for n in range(arrays):
            copies.append(
                pltpu.make_async_copy(refs[d].at[n], outs[n].at[:, lanes], sems.at[arrays * d + n])
            )
    for copy in copies:
        copy.start()
    for copy in copies:
        copy.wait()


def call(kernel, outs, ins, scratch=(), limit=56, where=ANY, cost=None, **kw):
    return pl.pallas_call(
        kernel,
        out_shape=outs,
        in_specs=ins,
        out_specs=[where] * len(outs),
        scratch_shapes=scratch,
        compiler_params=pltpu.CompilerParams(vmem_limit_bytes=limit * 2**20),
        cost_estimate=cost,
        **kw,
    )


def table_kernel(at, counts, rows, out):
    y, core, z = at[0], at[2], at[3]
    shape = rows.shape[1:]
    lane = lax.broadcasted_iota(jnp.int32, shape, 1)
    line = lax.broadcasted_iota(jnp.int32, shape, 0)
    spot = lax.broadcasted_iota(jnp.int32, (shape[0], SPOTS), 1)
    ahead = (
        lax.broadcasted_iota(jnp.int32, (128, 128), 0)
        < lax.broadcasted_iota(jnp.int32, (128, 128), 1)
    ).astype(F32)
    above = (
        lax.broadcasted_iota(jnp.int32, (shape[0], shape[0]), 1)
        < lax.broadcasted_iota(jnp.int32, (shape[0], shape[0]), 0)
    ).astype(F32)

    def at_least(a, *bounds):
        return sum((a >= b).astype(jnp.int32) for b in bounds)

    def slot(u):
        third = at_least(u, 3, 6, 9)
        return ((y - third) & 3) * 3 + u - 3 * third

    def place_values(rank, value, columns):
        made = jnp.zeros((shape[0], SPOTS), jnp.int32)
        for j in columns:
            made += jnp.where(rank[:, j : j + 1] == spot, value[:, j : j + 1], 0)
        return jnp.sum(made, 0, keepdims=True)

    for phase in range(2):
        kid = rows[0] if phase else jnp.where(core == 0, rows[1], rows[0])
        kept = jnp.zeros(shape, jnp.int32)
        for k in range(4 * PLANE):
            kept = jnp.where(kid == k, BLK - counts[k], kept)
        plane = at_least(kid, PLANE, 2 * PLANE, 3 * PLANE)
        t = kid - PLANE * plane
        half = at_least(t, HALF)
        listed = (
            at_least(kid, 0) * at_least(lane, 1) * (1 - at_least(lane, KPB)) * (1 - at_least(line, HALF))
        )
        here, same = (plane == z).astype(jnp.int32), (half == core).astype(jnp.int32)
        ks = slot(t - HALF * half)
        if phase:
            valid = listed * here * same
        else:
            above_it = (z < 3).astype(jnp.int32)
            valid = listed * jnp.where(core == 0, here * above_it, 1 - here * same)
            ks = ks + HALF * here * (1 - same)
        cls = jnp.clip(((kept + 31) >> 5) - 5, 0, 3)
        value = slot(line) | (ks << 4) | (kept << 9) | (cls << 18)
        rank, total = jnp.full(shape, -1, jnp.int32), 0
        for c in range(4):
            mine = valid * (cls == c).astype(jnp.int32)
            ones = mine.astype(F32)
            before = nn(ones, ahead) + jnp.sum(nn(above, ones), 1, keepdims=True)
            rank = jnp.where(mine > 0, total + before.astype(jnp.int32), rank)
            total = total + jnp.sum(mine)
        made = place_values(rank, value, range(1, KPB))
        first = spot[:1]
        made = jnp.where(first < total, made, HALF | (DUMMY[phase] << 4) | (3 << 18))
        out[phase : phase + 1] = jnp.where(first == SPOTS - 1, total, made)
        if phase:
            out[2:3] = place_values(jnp.where(line < HALF, slot(line), -1), kept, (0,))


def pairs_cost(pairs):
    return pl.CostEstimate(
        flops=pairs * 10 * BLK * BLK * HEAD, bytes_accessed=12 * 2**20, transcendentals=pairs * BLK * BLK
    )


def body(queries, keys, values, out_grad, key_blocks, target_counts):
    ctx, tp = lax.axis_index("ctx"), lax.axis_index("tp")
    z, x, y, core = ctx // 8, (ctx // 4) % 2, ctx % 4, tp % 2
    at = jnp.stack([y, x, core, z]).astype(jnp.int32)
    rows = queries.shape[0]
    shape = jax.ShapeDtypeStruct
    dma = lambda *n: pltpu.SemaphoreType.DMA(n)
    own = lax.dynamic_slice(key_blocks, (PLANE * z + HALF * core, 0), (HALF, KPB))
    after = lax.dynamic_slice(key_blocks, (jnp.minimum(PLANE * (z + 1), 84), 0), (HALF, KPB))
    lists = jnp.pad(jnp.stack([own, after]), ((0, 0), (0, 4), (0, 128 - KPB)), constant_values=-1)
    tab = call(
        table_kernel,
        [shape((3, SPOTS), jnp.int32)],
        [SMEM, SMEM, VMEM],
        where=VMEM,
        name="table",
    )(at, target_counts, lists)[0]
    half = shape((HALF, BLK, HEAD), BF)

    def split(first_round, *behind):
        return call(
            functools.partial(split_kernel, first_round),
            [shape((2, rows, HEAD), BF)] * 4,
            [SMEM] + [ANY] * (4 + len(behind)),
            [pltpu.VMEM((8, rows, HEAD), BF), dma(2, 8)],
            limit=56,
            name="split",
        )(at, queries, out_grad, keys, values, *behind)

    def send(pieces, pairs):
        return [lax.ppermute(p, AXES, pairs(d)) for d, p in enumerate(pieces)]

    two = shape((2, HALF, BLK, HEAD), BF)


    def blocks(pieces):
        return [p.reshape(2, 3, BLK, HEAD) for p in pieces]

    sent1 = split(True)
    sent2 = split(False, sent1[0], tab)
    r1 = blocks(send(sent1, to_heads))
    r2 = blocks(send(sent2, to_heads))
    first = call(
        gather_kernel,
        [two],
        [ANY] * 5,
        [pltpu.VMEM((4, 2, 3, BLK, HEAD), BF), dma(2, 4)],
        limit=40,
        name="gather",
    )(*r1, sent2[0])[0]
    across = lax.ppermute(first, AXES, ALONG_Z)
    near = call(
        gather_keys_kernel,
        [shape((2, n, BLK, HEAD), BF) for n in (MOST, HALF - MOST)],
        [SMEM] + [ANY] * 8,
        [pltpu.VMEM((HALF, 2, BLK, HEAD), BF), dma(2, HALF)],
        limit=40,
        name="gather_keys",
    )(at, *r1, *r2)
    near = [lax.ppermute(n, AXES, OTHER_CORE) for n in near]

    def scratch(k):
        return [
            pltpu.VMEM((HALF + 1, BLK, HEAD), BF),
            pltpu.VMEM((HALF + 1, BLK, HEAD), BF),
            pltpu.VMEM((k + 1, BLK, HEAD), BF),
            pltpu.VMEM((k + 1, BLK, HEAD), BF),
            pltpu.VMEM((HALF + 1, HEAD, BLK), F32),
            pltpu.VMEM((k + 1, BLK, HEAD), F32),
            pltpu.VMEM((k + 1, BLK, HEAD), F32),
        ]

    parts = [pltpu.VMEM((HALF, BLK, HEAD), BF)] * 5
    far, s1, beside = call(
        functools.partial(pairs_kernel, 0),
        [two, half, two],
        [SMEM] * 2 + [ANY] * 11,
        parts + scratch(PLANE) + [dma(44)],
        cost=pairs_cost(139),
        limit=56,
        name="far",
    )(at, tab, *r1, *r2, across, *near)
    back = lax.ppermute(far, AXES, BACK_Z)
    beside = lax.ppermute(beside, AXES, OTHER_CORE)
    dq, dk, dv = call(
        functools.partial(pairs_kernel, 1),
        [half, half, half],
        [SMEM] * 2 + [ANY] * 10,
        parts + scratch(HALF) + [dma(44)],
        cost=pairs_cost(60),
        limit=56,
        name="own",
    )(at, tab, *r1, *r2, s1, far)
    v3 = pltpu.VMEM((HALF, BLK, HEAD), BF)
    sums = call(
        sum_kernel,
        [shape((3, 3, BLK, HEAD), BF)] * 4,
        [SMEM] + [VMEM] * 2 + [ANY] * 3,
        [v3, v3, v3, pltpu.VMEM((4, 3, 3, BLK, HEAD), BF), dma(4, 3), dma(4)],
        limit=56,
        name="sums",
    )(at, beside, back, dq, dk, dv)
    back = send([p.reshape(3, rows, HEAD) for p in sums], from_heads)
    out = shape(queries.shape, BF)
    return tuple(
        call(
            functools.partial(join_kernel, 3),
            [out] * 3,
            [SMEM] + [VMEM] * 4,
            [dma(12)],
            limit=40,
            name="join",
        )(at, *back)
    )


def solution(mesh):
    in_specs = (P("ctx", "tp"),) * 4 + (P(), P())
    return jax.shard_map(
        body, mesh=mesh, in_specs=in_specs, out_specs=(P("ctx", "tp"),) * 3, check_vma=False
    )
```
